256 devices in a mesh: tm: 32 (over x, z), rows: 8 (over y, core).
Axes of the slice: x: 4, y: 4, z: 8, core: 2. Of those that a mesh axis runs over, the one named last changes fastest.
Arguments:
- queries: bfloat16 [64, 16, 80, 2240], P('tm', 'rows'), may hold values from -8 to 8
- key_rows: bfloat16 [64, 16, 80, 2240], P('tm', 'rows'), may hold values from -8 to 8
- value_rows: bfloat16 [64, 16, 80, 2240], P('tm', 'rows'), may hold values from -8 to 8
- hidden: bfloat16 [64, 16, 80, 5600], P('tm', 'rows'), may hold values from -6 to 6
- conv_weight: float32 [3, 3, 5600], replicated, may hold values from -2 to 2
- conv_bias: float32 [5600], replicated, may hold values from -2 to 2
Outputs:
- attended: float32 [64, 16, 80, 2240], P('tm', 'rows')
- gated: bfloat16 [64, 16, 80, 2800], P('tm', 'rows')
The draws below stay inside these ranges and needn't reach their ends.
All inputs are finite; a program needn't handle non-finite values.
Results may differ from the reference program's by a relative error of at most 0.0029.
Values may be sent and summed in bfloat16 or wider, within the bound.
A program may use at most 320 MiB of HBM per device.

```python
import jax
import jax.numpy as jnp
from jax import lax

HEADS = 20
HDIM = 112
FFW = 2800
WCOLS = 80
FRAMES = 64
LROWS = 16


def rough_field(key):
    first, second = jax.random.split(key)
    shape = (FRAMES, LROWS, WCOLS, HEADS * HDIM)
    base = jax.random.normal(first, shape, jnp.float32)
    spread = jnp.exp(jax.random.uniform(second, shape, jnp.float32, -1.5, 1.5))
    return base * spread


def shared_parts(key):
    key = jax.random.fold_in(key, 17)
    first, second, third = jax.random.split(key, 3)
    token_factor = jax.random.normal(first, (FRAMES, LROWS, WCOLS, HEADS, 1), jnp.float32)
    key_pattern = 0.5 + 0.6 * jax.random.normal(second, (HEADS, HDIM), jnp.float32)
    value_pattern = jax.random.normal(third, (HEADS, HDIM), jnp.float32)
    return (token_factor, key_pattern, value_pattern)


def draw_queries(key, part):
    key = jax.random.fold_in(key, 1)
    return jnp.clip(rough_field(key), -8.0, 8.0).astype(jnp.bfloat16)


def draw_key_rows(key, part):
    token_factor, key_pattern, value_pattern = shared_parts(key)
    key = jax.random.fold_in(key, 2)
    first, second, third = jax.random.split(key, 3)
    base = rough_field(first)
    frame_scale = jnp.exp(jax.random.uniform(second, (FRAMES, 1, 1, 1), jnp.float32, -1.0, 1.0))
    channel_offset = 0.8 * jax.random.normal(third, (HEADS * HDIM,), jnp.float32)
    common = (0.8 * token_factor * key_pattern).reshape(FRAMES, LROWS, WCOLS, HEADS * HDIM)
    return jnp.clip(base + frame_scale * channel_offset + common, -8.0, 8.0).astype(jnp.bfloat16)


def draw_value_rows(key, part):
    token_factor, key_pattern, value_pattern = shared_parts(key)
    key = jax.random.fold_in(key, 3)
    first, second = jax.random.split(key, 2)
    shape = (FRAMES, LROWS, WCOLS, HEADS * HDIM)
    noise = jax.random.normal(first, shape, jnp.float32)
    offset = jax.random.normal(second, (FRAMES, LROWS, 1, HEADS * HDIM), jnp.float32)
    common = (0.8 * token_factor * value_pattern).reshape(shape)
    return jnp.clip(noise + 1.5 * offset + common, -8.0, 8.0).astype(jnp.bfloat16)


def level_of(stream_key, extent, cuts, low, high):
    def one(axis_at, parts):
        steps = jax.random.uniform(jax.random.fold_in(jax.random.fold_in(stream_key, 6), axis_at), (parts,), jnp.float32, low / len(cuts), high / len(cuts))
        return jnp.repeat(jnp.exp(steps), extent[axis_at] // parts).reshape((-1,) + (1,) * (len(extent) - axis_at - 1))

    factor_of = one(*cuts[0])
    for cut in cuts[1:]:
        factor_of = factor_of * one(*cut)
    return factor_of


def centred(stream_key, shape, width, limit, cuts=(), held_as=jnp.bfloat16):
    entries = width * jax.random.normal(stream_key, shape, jnp.float32)
    if cuts:
        entries = entries * level_of(stream_key, shape, cuts, -0.22, 0.18)
    return jnp.clip(entries, -limit, limit).astype(held_as)


def setup_inputs(seed: int = 0) -> dict:
    key_of = jax.random.split(jax.random.key(seed), 7)
    return {
        "queries": draw_queries(jax.random.fold_in(key_of[6], 71), 0),
        "key_rows": draw_key_rows(jax.random.fold_in(key_of[6], 71), 0),
        "value_rows": draw_value_rows(jax.random.fold_in(key_of[6], 71), 0),
        "hidden": centred(key_of[3], (FRAMES, LROWS, WCOLS, 2 * FFW), 1.0, 6.0, ((0, 32), (1, 8))),
        "conv_weight": centred(key_of[4], (3, 3, 2 * FFW), 0.35, 2.0, (), jnp.float32),
        "conv_bias": centred(key_of[5], (2 * FFW,), 0.5, 2.0, (), jnp.float32),
    }


def features(block):
    return (jax.nn.elu(block.astype(jnp.float32)) + 1.0).astype(jnp.bfloat16)


def conv_frame(frame, conv_weight, conv_bias):
    padded = jnp.pad(frame, ((1, 1), (1, 1), (0, 0)))
    accum = jnp.zeros(frame.shape, jnp.float32) + conv_bias
    for i in range(3):
        for j in range(3):
            accum = accum + padded[i:i + LROWS, j:j + WCOLS].astype(jnp.float32) * conv_weight[i, j]
    return (accum[..., :FFW] * jax.nn.silu(accum[..., FFW:])).astype(jnp.bfloat16)


def reference(queries, key_rows, value_rows, hidden, conv_weight, conv_bias):
    shape = (FRAMES, LROWS * WCOLS, HEADS, HDIM)
    phi_query = features(queries).reshape(shape)
    phi_key = features(key_rows).reshape(shape)
    value_heads = value_rows.reshape(shape)

    def advance(carry, frame):
        state, total = carry
        query_f, key_f, value_f = frame
        state = state + jnp.einsum('thd,the->hde', key_f.astype(jnp.float32), value_f.astype(jnp.float32))
        total = total + jnp.sum(key_f.astype(jnp.float32), axis=0)
        state_low = state.astype(jnp.bfloat16)
        numerator = jnp.einsum('thd,hde->the', query_f.astype(jnp.float32), state_low.astype(jnp.float32))
        denominator = jnp.einsum('thd,hd->th', query_f.astype(jnp.float32), total)
        return (state, total), numerator / denominator[..., None]

    start = (jnp.zeros((HEADS, HDIM, HDIM), jnp.float32), jnp.zeros((HEADS, HDIM), jnp.float32))
    ignored, outputs = lax.scan(advance, start, (phi_query, phi_key, value_heads))
    attended = outputs.reshape(FRAMES, LROWS, WCOLS, HEADS * HDIM)
    gated = lax.map(lambda frame: conv_frame(frame, conv_weight, conv_bias), hidden)
    return attended, gated
```

```python
import jax
import jax.numpy as jnp
from jax import lax
from jax.experimental import pallas as pl
from jax.experimental.pallas import tpu as pltpu
from jax.sharding import PartitionSpec as P

HEADS = 20
HDIM = 112
WIDTH = HEADS * HDIM
HALF = 2800
FULL = 2 * HALF
COLS = 80
TOK = 2 * COLS
LT = 18
LPAD = LT * 128
HT = LT // 2
BLK = 1024
TOTROW = HT * HDIM
QTR = BLK // 4
SL = QTR // 8
MESH = pl.DeviceIdType.MESH
CUTS = (0, 4, 8, 12, 16, 19, 22)
NP = len(CUTS) - 1


def val_lanes(k):
    lo, hi = CUTS[k], min(CUTS[k + 1], 21)
    return lo * 128, (hi - lo) * 128


def gate_lanes(k):
    lo = 21 if k == 0 else 22 + CUTS[k]
    hi = min(22 + CUTS[k + 1], 44)
    start, end = lo * 128, min(hi * 128, FULL)
    return start, end - start


def features(x):
    x = x.astype(jnp.float32)
    return jnp.where(x > 0, x + 1.0, jnp.exp(x)).astype(jnp.bfloat16)


def kernel(
    q_hbm, k_hbm, v_hbm, h_hbm, w_hbm, b_hbm,
    att_hbm, gat_hbm,
    q_v, k_v, v_v, h_v, w_v, b_v, up_v, dn_v,
    dense, state, send_c, recv_c, send_a, recv_a, send_b, recv_b, own,
    send_z, recv_z, send_x, recv_x, send_e, recv_e, final, wide, att_v, gat_v,
    load_sem, kv_sem, out_sem, halo_s, halo_r, c_s, c_r, a_s, a_r, b_s, b_r,
    z_s, z_r, x_s, x_r, e_s, e_r, g_s, g_r, f_s, f_r,
):
    tm = lax.axis_index("tm")
    row = lax.axis_index("rows")
    x, z = tm // 8, tm % 8
    y, c = row // 2, row % 2
    sib = (tm, row + 1 - 2 * c)
    alpha = y + 1 - 2 * (y % 2)
    beta = 3 - y
    opp = (y + 2) % 4
    dev_a, dev_b = (tm, alpha * 2 + c), (tm, beta * 2 + c)
    above, below = (tm, (row + 7) % 8), (tm, (row + 1) % 8)
    zdev = [(x * 8 + (z + d) % 8, row) for d in range(8)]
    xdev = [(((x + d) % 4) * 8 + z, row) for d in range(4)]

    def load(src, dst, sem):
        copy = pltpu.make_async_copy(src, dst, sem)
        copy.start()
        return copy

    kv = [
        (load(k_hbm.at[f], k_v.at[f], kv_sem.at[f, 0]), load(v_hbm.at[f], v_v.at[f], kv_sem.at[f, 1]))
        for f in range(2)
    ]
    load_h = load(h_hbm, h_v, load_sem.at[0])
    load_q = load(q_hbm, q_v, load_sem.at[1])
    load_w = load(w_hbm, w_v, load_sem.at[2])
    load_b = load(b_hbm, b_v, load_sem.at[3])

    barrier = pltpu.get_barrier_semaphore()
    partners = [above, below, dev_a, dev_b] + zdev[1:] + xdev[1:]
    for device in partners:
        pl.semaphore_signal(barrier, inc=1, device_id=device, device_id_type=MESH)
    pl.semaphore_wait(barrier, len(partners))

    def remote(src, dst, ss, rs, device):
        return pltpu.make_async_remote_copy(
            src_ref=src, dst_ref=dst, send_sem=ss, recv_sem=rs, device_id=device, device_id_type=MESH
        )

    def halo(k):
        copies = []
        for n, (start, size) in enumerate((val_lanes(k), gate_lanes(k))):
            lanes = pl.ds(start, size)
            copies.append(remote(h_hbm.at[:, 1, :, lanes], up_v.at[:, :, lanes],
                                 halo_s.at[k, n, 0], halo_r.at[k, n, 0], below))
            copies.append(remote(h_hbm.at[:, 0, :, lanes], dn_v.at[:, :, lanes],
                                 halo_s.at[k, n, 1], halo_r.at[k, n, 1], above))
        return copies

    halos = [halo(k) for k in range(NP)]

    def start(copies):
        for copy in copies:
            copy.start()

    for k in range(NP):
        start(halos[k])

    lane = lax.broadcasted_iota(jnp.int32, (HDIM, 2 * HDIM), 1)
    sends = []
    core = []
    for f in range(2):
        kv[f][0].wait()
        kv[f][1].wait()
        phi = features(k_v[f].reshape(TOK, WIDTH))
        val = v_v[f].reshape(TOK, WIDTH)
        dense[:, LPAD - 128:] = jnp.zeros((HDIM, 128), jnp.float32)
        for p in range(HEADS // 2):
            lo = 2 * HDIM * p
            prod = lax.dot_general(
                phi[:, lo:lo + 2 * HDIM], val[:, lo:lo + 2 * HDIM], (((0,), (0,)), ((), ())),
                preferred_element_type=jnp.float32,
            )
            dense[:, lo:lo + 2 * HDIM] = jnp.where(lane < HDIM, prod[:HDIM], prod[HDIM:])
        total = jnp.sum(phi.astype(jnp.float32), axis=0, keepdims=True)
        total = jnp.concatenate([total, jnp.zeros((1, LPAD - WIDTH), jnp.float32)], axis=1)
        for l in range(LT):
            half, at = l // HT, l % HT
            state[f, half, at * HDIM:(at + 1) * HDIM] = dense[:, l * 128:(l + 1) * 128]
        for half in range(2):
            rows = [total[:, l * 128:(l + 1) * 128] for l in range(half * HT, (half + 1) * HT)]
            rows.append(jnp.zeros((BLK - TOTROW - HT, 128), jnp.float32))
            state[f, half, TOTROW:] = jnp.concatenate(rows, axis=0)
        send_c[f] = state[f, 1 - c].astype(jnp.bfloat16)
        copy = remote(send_c.at[f], recv_c.at[f], c_s.at[f], c_r.at[f], sib)
        copy.start()
        core.append(copy)

    load_h.wait()
    load_w.wait()
    load_b.wait()
    top = jnp.where(row > 0, 1.0, 0.0)
    bottom = jnp.where(row < 7, 1.0, 0.0)
    shift = FULL - HALF - 22 * 128 + 128
    col8 = lax.broadcasted_iota(jnp.int32, (8, 128), 0)

    def conv_tile(f, src, n, take):
        rows = [up_v[f, :, src], h_v[f, 0, :, src], h_v[f, 1, :, src], dn_v[f, :, src]]
        rows = [take(r).astype(jnp.float32) for r in rows]
        bias = take(b_v[:, src])
        weight = [take(w_v[i, :, src]) for i in range(3)]
        first, last = [weight[0] * top, weight[1], weight[2]], [weight[0], weight[1], weight[2] * bottom]
        outs = []
        for o, weights in ((0, first), (1, last)):
            parts = []
            for j in range(3):
                parts.append(sum(rows[o + i] * weights[i][j:j + 1] for i in range(3)))
            edge = col8[:, :n]
            left = jnp.concatenate([parts[0][:72], jnp.where(edge < 7, parts[0][72:], 0.0)], axis=0)
            right = jnp.concatenate([jnp.where(edge > 0, parts[2][:8], 0.0), parts[2][8:]], axis=0)
            outs.append(parts[1] + bias + pltpu.roll(left, 1, 0) + pltpu.roll(right, COLS - 1, 0))
        return outs

    def conv_out(f, a, n):
        gate_at = (21 + a) * 128
        if n == 128:
            gate_src = pl.ds(pl.multiple_of(gate_at, 128), 256)
            value_src = pl.ds(pl.multiple_of(a * 128, 128), 128)
        else:
            gate_src = pl.ds(gate_at, FULL - gate_at)
            value_src = pl.ds(a * 128, 128)
        gate = conv_tile(f, gate_src, n, lambda r: r[:, shift:shift + n])
        value = conv_tile(f, value_src, n, lambda r: r[:, :n])
        for o in range(2):
            gated = value[o] * (gate[o] / (1.0 + jnp.exp(-gate[o])))
            gat_v[f, o, :, pl.ds(a * 128 if n < 128 else pl.multiple_of(a * 128, 128), n)] = gated.astype(jnp.bfloat16)

    def conv(k):
        for copy in halos[k]:
            copy.wait_recv()
        lo, hi = CUTS[k], min(CUTS[k + 1], 21)

        @pl.loop(0, 2)
        def _(f):
            @pl.loop(lo, hi)
            def _(a):
                conv_out(f, a, 128)

            if CUTS[k + 1] == 22:
                conv_out(f, 21, HALF - 21 * 128)

    hops = ((alpha, dev_a, beta, dev_b), (beta, dev_b, alpha, dev_a))

    def quarter(q):
        return pl.ds(pl.multiple_of(q * QTR, QTR), QTR)

    step_a = []
    for f in range(2):
        first, dev, second, _ = hops[f]
        core[f].wait_recv()
        for n, q in ((0, first), (1, opp)):
            send_a[f, n] = (state[f, c, quarter(q)] + recv_c[f, quarter(q)].astype(jnp.float32)).astype(jnp.bfloat16)
        copy = remote(send_a.at[f], recv_a.at[f], a_s.at[f], a_r.at[f], dev)
        copy.start()
        step_a.append(copy)
    conv(0)
    step_b = []
    for f in range(2):
        first, _, second, dev = hops[f]
        step_a[f].wait_recv()
        q = quarter(second)
        send_b[f] = (state[f, c, q] + recv_c[f, q].astype(jnp.float32) + recv_a[f, 1].astype(jnp.float32)).astype(jnp.bfloat16)
        copy = remote(send_b.at[f], recv_b.at[f], b_s.at[f], b_r.at[f], dev)
        copy.start()
        step_b.append(copy)
        q = quarter(y)
        own[f] = state[f, c, q] + recv_c[f, q].astype(jnp.float32) + recv_a[f, 0].astype(jnp.float32)
    conv(1)
    for f in range(2):
        step_b[f].wait_recv()
        own[f] = own[f] + recv_b[f].astype(jnp.float32)

    send_z[...] = (own[0] + own[1]).astype(jnp.bfloat16).reshape(8, SL, 128)
    step_z = []
    for d in (4, 3, 5, 2, 6, 1, 7):
        copy = remote(send_z.at[(z + d) % 8], recv_z.at[z], z_s.at[d - 1], z_r.at[d - 1], zdev[d])
        copy.start()
        step_z.append(copy)
    recv_z[z] = send_z[z]
    conv(2)
    for copy in step_z:
        copy.wait_recv()
    send_x[...] = sum(recv_z[j].astype(jnp.float32) for j in range(8)).astype(jnp.bfloat16)
    step_x = []
    for d in (2, 1, 3):
        copy = remote(send_x, recv_x.at[x], x_s.at[d - 1], x_r.at[d - 1], xdev[d])
        copy.start()
        step_x.append(copy)
    recv_x[x] = jnp.zeros((SL, 128), jnp.bfloat16)
    conv(3)
    for copy in step_x:
        copy.wait_recv()
    running = jnp.zeros((SL, 128), jnp.float32)
    for i in range(4):
        running = running + jnp.where(i < x, recv_x[i].astype(jnp.float32), 0.0)
    for j in range(8):
        send_e[j] = running.astype(jnp.bfloat16)
        running = running + recv_z[j].astype(jnp.float32)
    step_e = []
    for d in (4, 3, 5, 2, 6, 1, 7):
        copy = remote(send_e.at[(z + d) % 8], recv_e.at[z], e_s.at[d - 1], e_r.at[d - 1], zdev[d])
        copy.start()
        step_e.append(copy)
    recv_e[z] = send_e[z]
    load_q.wait()
    conv(4)
    for copy in step_e:
        copy.wait_recv()

    before = recv_e[...].reshape(QTR, 128).astype(jnp.float32)
    states = before + own[0]
    final[0, c, quarter(y)] = states.astype(jnp.bfloat16)
    final[1, c, quarter(y)] = (states + own[1]).astype(jnp.bfloat16)

    forwards = [[], []]

    def spread(f, q, dev, ss, rs):
        ref = final.at[f, c, quarter(q)]
        copy = remote(ref, ref, ss, rs, dev)
        copy.start()
        return copy

    def forward(f, q):
        n = len(forwards[f])
        forwards[f].append(spread(f, q, sib, f_s.at[f, n], f_r.at[f, n]))

    step_g = [[], []]
    for f in range(2):
        first, dev1, second, dev2 = hops[f]
        step_g[f].append(spread(f, y, dev2, g_s.at[f, 0], g_r.at[f, 0]))
        step_g[f].append(spread(f, y, dev1, g_s.at[f, 1], g_r.at[f, 1]))
    for f in range(2):
        forward(f, y)
    for f in range(2):
        first, dev1, second, dev2 = hops[f]
        step_g[f][0].wait_recv()
        step_g[f].append(spread(f, second, dev1, g_s.at[f, 2], g_r.at[f, 2]))
        forward(f, second)
    conv(5)
    for f in range(2):
        first, dev1, second, dev2 = hops[f]
        step_g[f][1].wait_recv()
        forward(f, first)
    for f in range(2):
        step_g[f][2].wait_recv()
        forward(f, opp)
    out_g = load(gat_v, gat_hbm, out_sem.at[0])

    same = (lax.broadcasted_iota(jnp.int32, (2 * HDIM, 2 * HDIM), 0) < HDIM) == (
        lax.broadcasted_iota(jnp.int32, (2 * HDIM, 2 * HDIM), 1) < HDIM
    )
    ones = jnp.where(same, 1.0, 0.0).astype(jnp.bfloat16)
    out_a = []
    for f in range(2):
        for copy in forwards[f]:
            copy.wait_recv()
        for l in range(LT):
            half, at = l // HT, l % HT
            wide[:, l * 128:(l + 1) * 128] = final[f, half, at * HDIM:(at + 1) * HDIM]
        tails = [final[f, half, TOTROW:].astype(jnp.float32) for half in range(2)]
        total = jnp.concatenate([tails[l // HT][l % HT:l % HT + 1] for l in range(LT)], axis=1)[:, :WIDTH]
        phi = features(q_v[f].reshape(TOK, WIDTH))
        scaled = (phi.astype(jnp.float32) * total).astype(jnp.bfloat16)
        for p in range(HEADS // 2):
            lo = 2 * HDIM * p
            block = wide[:, lo:lo + 2 * HDIM]
            block = jnp.concatenate([block, block], axis=0)
            block = jnp.where(same, block, jnp.zeros_like(block))
            num = jnp.dot(phi[:, lo:lo + 2 * HDIM], block, preferred_element_type=jnp.float32)
            den = jnp.dot(scaled[:, lo:lo + 2 * HDIM], ones, preferred_element_type=jnp.float32)
            att_v[f, :, :, lo:lo + 2 * HDIM] = (num / den).reshape(2, COLS, 2 * HDIM)
        out_a.append(load(att_v.at[f], att_hbm.at[f], out_sem.at[1 + f]))

    for copies in halos + [core, step_a, step_b, step_z, step_x, step_e] + step_g + forwards:
        for copy in copies:
            copy.wait_send()
    out_g.wait()
    for copy in out_a:
        copy.wait()


def on_device(queries, key_rows, value_rows, hidden, conv_weight, conv_bias):
    bf, f32 = jnp.bfloat16, jnp.float32
    vmem, dma = pltpu.VMEM, pltpu.SemaphoreType.DMA
    hbm = pl.BlockSpec(memory_space=pl.ANY)
    return pl.pallas_call(
        kernel,
        out_shape=(
            jax.ShapeDtypeStruct((2, 2, COLS, WIDTH), f32),
            jax.ShapeDtypeStruct((2, 2, COLS, HALF), bf),
        ),
        in_specs=[hbm] * 6,
        out_specs=(hbm, hbm),
        scratch_shapes=[
            vmem((2, 2, COLS, WIDTH), bf), vmem((2, 2, COLS, WIDTH), bf), vmem((2, 2, COLS, WIDTH), bf),
            vmem((2, 2, COLS, FULL), bf), vmem((3, 3, FULL), f32), vmem((1, FULL), f32),
            vmem((2, COLS, FULL), bf), vmem((2, COLS, FULL), bf),
            vmem((HDIM, LPAD), f32), vmem((2, 2, BLK, 128), f32),
            vmem((2, BLK, 128), bf), vmem((2, BLK, 128), bf),
            vmem((2, 2, QTR, 128), bf), vmem((2, 2, QTR, 128), bf),
            vmem((2, QTR, 128), bf), vmem((2, QTR, 128), bf), vmem((2, QTR, 128), f32),
            vmem((8, SL, 128), bf), vmem((8, SL, 128), bf),
            vmem((SL, 128), bf), vmem((4, SL, 128), bf),
            vmem((8, SL, 128), bf), vmem((8, SL, 128), bf),
            vmem((2, 2, BLK, 128), bf), vmem((HDIM, LPAD), bf),
            vmem((2, 2, COLS, WIDTH), f32), vmem((2, 2, COLS, HALF), bf),
            dma((4,)), dma((2, 2)), dma((3,)), dma((NP, 2, 2)), dma((NP, 2, 2)),
            dma((2,)), dma((2,)), dma((2,)), dma((2,)), dma((2,)), dma((2,)),
            dma((7,)), dma((7,)), dma((3,)), dma((3,)), dma((7,)), dma((7,)),
            dma((2, 3)), dma((2, 3)), dma((2, 4)), dma((2, 4)),
        ],
        compiler_params=pltpu.CompilerParams(
            collective_id=0, has_side_effects=True, vmem_limit_bytes=48 * 1024 * 1024
        ),
        name="linear_attention_conv",
    )(queries, key_rows, value_rows, hidden, conv_weight, conv_bias.reshape(1, FULL))


def solution(mesh):
    block = P("tm", "rows", None, None)
    return jax.shard_map(
        on_device, mesh=mesh, in_specs=(block, block, block, block, P(), P()),
        out_specs=(block, block), check_vma=False,
    )
```

```python
import jax
import jax.numpy as jnp
from jax import lax
from jax.experimental import pallas as pl
from jax.experimental.pallas import tpu as pltpu
from jax.sharding import PartitionSpec as P

HEADS = 20
HDIM = 112
WIDTH = HEADS * HDIM
HALF = 2800
FULL = 2 * HALF
COLS = 80
TOK = 2 * COLS
LT = 18
LPAD = LT * 128
HT = LT // 2
BLK = 1024
TOTROW = HT * HDIM
QTR = BLK // 4
SL = QTR // 8
MESH = pl.DeviceIdType.MESH
CUTS = (0, 4, 8, 12, 16, 19, 22)
NP = len(CUTS) - 1
VMEM_BYTES = 56 * 1024 * 1024


def val_lanes(k):
    lo, hi = CUTS[k], min(CUTS[k + 1], 21)
    return lo * 128, (hi - lo) * 128


def gate_lanes(k):
    lo = 21 if k == 0 else 22 + CUTS[k]
    hi = min(22 + CUTS[k + 1], 44)
    start, end = lo * 128, min(hi * 128, FULL)
    return start, end - start


def features(x):
    x = x.astype(jnp.float32)
    return jnp.where(x > 0, x + 1.0, jnp.exp(x)).astype(jnp.bfloat16)


def kernel(
    q_hbm, k_hbm, v_hbm, h_hbm, w_hbm, b_hbm,
    final, phi_v, gat_v,
    q_v, k_v, v_v, h_v, w_v, b_v, up_v, dn_v,
    dense, state, send_c, recv_c, send_a, recv_a, send_b, recv_b, own,
    send_z, recv_z, send_x, recv_x, send_e, recv_e,
    load_sem, kv_sem, halo_s, halo_r, c_s, c_r, a_s, a_r, b_s, b_r,
    z_s, z_r, x_s, x_r, e_s, e_r, g_s, g_r, f_s, f_r,
):
    tm = lax.axis_index("tm")
    row = lax.axis_index("rows")
    x, z = tm // 8, tm % 8
    y, c = row // 2, row % 2
    sib = (tm, row + 1 - 2 * c)
    alpha = y + 1 - 2 * (y % 2)
    beta = 3 - y
    opp = (y + 2) % 4
    dev_a, dev_b = (tm, alpha * 2 + c), (tm, beta * 2 + c)
    above, below = (tm, (row + 7) % 8), (tm, (row + 1) % 8)
    zdev = [(x * 8 + (z + d) % 8, row) for d in range(8)]
    xdev = [(((x + d) % 4) * 8 + z, row) for d in range(4)]

    def load(src, dst, sem):
        copy = pltpu.make_async_copy(src, dst, sem)
        copy.start()
        return copy

    kv = [
        (load(k_hbm.at[f], k_v.at[f], kv_sem.at[f, 0]), load(v_hbm.at[f], v_v.at[f], kv_sem.at[f, 1]))
        for f in range(2)
    ]
    load_h = load(h_hbm, h_v, load_sem.at[0])
    load_q = load(q_hbm, q_v, load_sem.at[1])
    load_w = load(w_hbm, w_v, load_sem.at[2])
    load_b = load(b_hbm, b_v.at[0], load_sem.at[3])

    barrier = pltpu.get_barrier_semaphore()
    partners = [above, below, dev_a, dev_b] + zdev[1:] + xdev[1:]
    for device in partners:
        pl.semaphore_signal(barrier, inc=1, device_id=device, device_id_type=MESH)

    def remote(src, dst, ss, rs, device):
        return pltpu.make_async_remote_copy(
            src_ref=src, dst_ref=dst, send_sem=ss, recv_sem=rs, device_id=device, device_id_type=MESH
        )

    def halo(k):
        copies = []
        for n, (start, size) in enumerate((val_lanes(k), gate_lanes(k))):
            lanes = pl.ds(start, size)
            copies.append(remote(h_hbm.at[:, 1, :, lanes], up_v.at[:, :, lanes],
                                 halo_s.at[k, n, 0], halo_r.at[k, n, 0], below))
            copies.append(remote(h_hbm.at[:, 0, :, lanes], dn_v.at[:, :, lanes],
                                 halo_s.at[k, n, 1], halo_r.at[k, n, 1], above))
        return copies

    halos = [halo(k) for k in range(NP)]

    def start(copies):
        for copy in copies:
            copy.start()

    lane = lax.broadcasted_iota(jnp.int32, (HDIM, 2 * HDIM), 1)
    sends = []
    core = []
    for f in range(2):
        kv[f][0].wait()
        kv[f][1].wait()
        if f == 0:
            pl.semaphore_wait(barrier, len(partners))
            start(halos[0])
            start(halos[1])
        phi = features(k_v[f].reshape(TOK, WIDTH))
        val = v_v[f].reshape(TOK, WIDTH)
        dense[:, LPAD - 128:] = jnp.zeros((HDIM, 128), jnp.float32)
        for p in range(HEADS // 2):
            lo = 2 * HDIM * p
            prod = lax.dot_general(
                phi[:, lo:lo + 2 * HDIM], val[:, lo:lo + 2 * HDIM], (((0,), (0,)), ((), ())),
                preferred_element_type=jnp.float32,
            )
            dense[:, lo:lo + 2 * HDIM] = jnp.where(lane < HDIM, prod[:HDIM], prod[HDIM:])
        total = jnp.sum(phi.astype(jnp.float32), axis=0, keepdims=True)
        total = jnp.concatenate([total, jnp.zeros((1, LPAD - WIDTH), jnp.float32)], axis=1)
        for l in range(LT):
            half, at = l // HT, l % HT
            state[f, half, at * HDIM:(at + 1) * HDIM] = dense[:, l * 128:(l + 1) * 128]
        for half in range(2):
            rows = [total[:, l * 128:(l + 1) * 128] for l in range(half * HT, (half + 1) * HT)]
            rows.append(jnp.zeros((BLK - TOTROW - HT, 128), jnp.float32))
            state[f, half, TOTROW:] = jnp.concatenate(rows, axis=0)
        send_c[f] = state[f, 1 - c].astype(jnp.bfloat16)
        copy = remote(send_c.at[f], recv_c.at[f], c_s.at[f], c_r.at[f], sib)
        copy.start()
        core.append(copy)

    load_h.wait()
    load_w.wait()
    load_b.wait()
    top = jnp.where(row > 0, 1.0, 0.0)
    bottom = jnp.where(row < 7, 1.0, 0.0)
    shift = FULL - HALF - 22 * 128 + 128
    col8 = lax.broadcasted_iota(jnp.int32, (8, 128), 0)

    def conv_tile(f, src, n, take):
        rows = [up_v[f, :, src], h_v[f, 0, :, src], h_v[f, 1, :, src], dn_v[f, :, src]]
        rows = [take(r).astype(jnp.float32) for r in rows]
        bias = take(b_v[:, src])
        weight = [take(w_v[i, :, src]) for i in range(3)]
        first, last = [weight[0] * top, weight[1], weight[2]], [weight[0], weight[1], weight[2] * bottom]
        outs = []
        for o, weights in ((0, first), (1, last)):
            parts = []
            for j in range(3):
                parts.append(sum(rows[o + i] * weights[i][j:j + 1] for i in range(3)))
            edge = col8[:, :n]
            left = jnp.concatenate([parts[0][:72], jnp.where(edge < 7, parts[0][72:], 0.0)], axis=0)
            right = jnp.concatenate([jnp.where(edge > 0, parts[2][:8], 0.0), parts[2][8:]], axis=0)
            outs.append(parts[1] + bias + pltpu.roll(left, 1, 0) + pltpu.roll(right, COLS - 1, 0))
        return outs

    def conv_out(f, a, n):
        gate_at = (21 + a) * 128
        if n == 128:
            gate_src = pl.ds(pl.multiple_of(gate_at, 128), 256)
            value_src = pl.ds(pl.multiple_of(a * 128, 128), 128)
        else:
            gate_src = pl.ds(gate_at, FULL - gate_at)
            value_src = pl.ds(a * 128, 128)
        gate = conv_tile(f, gate_src, n, lambda r: r[:, shift:shift + n])
        value = conv_tile(f, value_src, n, lambda r: r[:, :n])
        for o in range(2):
            gated = value[o] * (gate[o] / (1.0 + jnp.exp(-gate[o])))
            gat_v[f, o, :, pl.ds(a * 128 if n < 128 else pl.multiple_of(a * 128, 128), n)] = gated.astype(jnp.bfloat16)

    def conv(k):
        for copy in halos[k]:
            copy.wait_recv()
        lo, hi = CUTS[k], min(CUTS[k + 1], 21)

        @pl.loop(0, 2)
        def _(f):
            @pl.loop(lo, hi)
            def _(a):
                conv_out(f, a, 128)

            if CUTS[k + 1] == 22:
                conv_out(f, 21, HALF - 21 * 128)

    hops = ((alpha, dev_a, beta, dev_b), (beta, dev_b, alpha, dev_a))

    def quarter(q):
        return pl.ds(pl.multiple_of(q * QTR, QTR), QTR)

    step_a = []
    for f in range(2):
        first, dev, second, _ = hops[f]
        core[f].wait_recv()
        for n, q in ((0, first), (1, opp)):
            send_a[f, n] = (state[f, c, quarter(q)] + recv_c[f, quarter(q)].astype(jnp.float32)).astype(jnp.bfloat16)
        copy = remote(send_a.at[f], recv_a.at[f], a_s.at[f], a_r.at[f], dev)
        copy.start()
        step_a.append(copy)
    conv(0)
    step_b = []
    for f in range(2):
        first, _, second, dev = hops[f]
        step_a[f].wait_recv()
        q = quarter(second)
        send_b[f] = (state[f, c, q] + recv_c[f, q].astype(jnp.float32) + recv_a[f, 1].astype(jnp.float32)).astype(jnp.bfloat16)
        copy = remote(send_b.at[f], recv_b.at[f], b_s.at[f], b_r.at[f], dev)
        copy.start()
        step_b.append(copy)
        q = quarter(y)
        own[f] = state[f, c, q] + recv_c[f, q].astype(jnp.float32) + recv_a[f, 0].astype(jnp.float32)
    load_q.wait()
    for f in range(2):
        for r in range(2):
            phi_v[f, r] = features(q_v[f, r])
    for f in range(2):
        step_b[f].wait_recv()
        own[f] = own[f] + recv_b[f].astype(jnp.float32)

    send_z[...] = (own[0] + own[1]).astype(jnp.bfloat16).reshape(8, SL, 128)
    step_z = []
    for d in (4, 3, 5, 2, 6, 1, 7):
        copy = remote(send_z.at[(z + d) % 8], recv_z.at[z], z_s.at[d - 1], z_r.at[d - 1], zdev[d])
        copy.start()
        step_z.append(copy)
    recv_z[z] = send_z[z]
    for k in range(2, NP):
        start(halos[k])
    conv(1)
    for copy in step_z:
        copy.wait_recv()
    send_x[...] = sum(recv_z[j].astype(jnp.float32) for j in range(8)).astype(jnp.bfloat16)
    step_x = []
    for d in (2, 1, 3):
        copy = remote(send_x, recv_x.at[x], x_s.at[d - 1], x_r.at[d - 1], xdev[d])
        copy.start()
        step_x.append(copy)
    recv_x[x] = jnp.zeros((SL, 128), jnp.bfloat16)
    conv(2)
    for copy in step_x:
        copy.wait_recv()
    running = jnp.zeros((SL, 128), jnp.float32)
    for i in range(4):
        running = running + jnp.where(i < x, recv_x[i].astype(jnp.float32), 0.0)
    for j in range(8):
        send_e[j] = running.astype(jnp.bfloat16)
        running = running + recv_z[j].astype(jnp.float32)
    step_e = []
    for d in (4, 3, 5, 2, 6, 1, 7):
        copy = remote(send_e.at[(z + d) % 8], recv_e.at[z], e_s.at[d - 1], e_r.at[d - 1], zdev[d])
        copy.start()
        step_e.append(copy)
    recv_e[z] = send_e[z]
    conv(3)
    for copy in step_e:
        copy.wait_recv()

    before = recv_e[...].reshape(QTR, 128).astype(jnp.float32)
    states = before + own[0]
    final[0, c, quarter(y)] = states.astype(jnp.bfloat16)
    final[1, c, quarter(y)] = (states + own[1]).astype(jnp.bfloat16)

    forwards = [[], []]

    def spread(f, q, dev, ss, rs):
        ref = final.at[f, c, quarter(q)]
        copy = remote(ref, ref, ss, rs, dev)
        copy.start()
        return copy

    def forward(f, q):
        n = len(forwards[f])
        forwards[f].append(spread(f, q, sib, f_s.at[f, n], f_r.at[f, n]))

    step_g = [[], []]
    for f in range(2):
        first, dev1, second, dev2 = hops[f]
        step_g[f].append(spread(f, y, dev2, g_s.at[f, 0], g_r.at[f, 0]))
        step_g[f].append(spread(f, y, dev1, g_s.at[f, 1], g_r.at[f, 1]))
    for f in range(2):
        forward(f, y)
    for f in range(2):
        first, dev1, second, dev2 = hops[f]
        step_g[f][0].wait_recv()
        step_g[f].append(spread(f, second, dev1, g_s.at[f, 2], g_r.at[f, 2]))
        forward(f, second)
    conv(4)
    for f in range(2):
        first, dev1, second, dev2 = hops[f]
        step_g[f][1].wait_recv()
        forward(f, first)
    for f in range(2):
        step_g[f][2].wait_recv()
        forward(f, opp)
    conv(5)

    for f in range(2):
        for copy in forwards[f]:
            copy.wait_recv()
    for copies in halos + [core, step_a, step_b, step_z, step_x, step_e] + step_g + forwards:
        for copy in copies:
            copy.wait_send()


def attend(phi_v, state_in, gat_v, att_out, gat_out, wide, att_v, sem):
    copy_g = pltpu.make_async_copy(gat_v, gat_out, sem.at[0])
    copy_g.start()
    same = (lax.broadcasted_iota(jnp.int32, (2 * HDIM, 2 * HDIM), 0) < HDIM) == (
        lax.broadcasted_iota(jnp.int32, (2 * HDIM, 2 * HDIM), 1) < HDIM
    )
    ones = jnp.where(same, 1.0, 0.0).astype(jnp.bfloat16)
    outs = []
    for f in range(2):
        for l in range(LT):
            half, at = l // HT, l % HT
            wide[:, l * 128:(l + 1) * 128] = state_in[f, half, at * HDIM:(at + 1) * HDIM]
        tails = [state_in[f, half, TOTROW:].astype(jnp.float32) for half in range(2)]
        total = jnp.concatenate([tails[l // HT][l % HT:l % HT + 1] for l in range(LT)], axis=1)[:, :WIDTH]
        phi = phi_v[f].reshape(TOK, WIDTH)
        scaled = (phi.astype(jnp.float32) * total).astype(jnp.bfloat16)
        for p in range(HEADS // 2):
            lo = 2 * HDIM * p
            block = wide[:, lo:lo + 2 * HDIM]
            block = jnp.concatenate([block, block], axis=0)
            block = jnp.where(same, block, jnp.zeros_like(block))
            num = jnp.dot(phi[:, lo:lo + 2 * HDIM], block, preferred_element_type=jnp.float32)
            den = jnp.dot(scaled[:, lo:lo + 2 * HDIM], ones, preferred_element_type=jnp.float32)
            att_v[f, :, :, lo:lo + 2 * HDIM] = (num / den).reshape(2, COLS, 2 * HDIM)
        copy = pltpu.make_async_copy(att_v.at[f], att_out.at[f], sem.at[1 + f])
        copy.start()
        outs.append(copy)
    copy_g.wait()
    for copy in outs:
        copy.wait()


def on_device(queries, key_rows, value_rows, hidden, conv_weight, conv_bias):
    bf, f32 = jnp.bfloat16, jnp.float32
    vmem, dma = pltpu.VMEM, pltpu.SemaphoreType.DMA
    hbm = pl.BlockSpec(memory_space=pltpu.HBM)
    states, phi, gated = pl.pallas_call(
        kernel,
        out_shape=(
            vmem((2, 2, BLK, 128), bf), vmem((2, 2, COLS, WIDTH), bf), vmem((2, 2, COLS, HALF), bf),
        ),
        in_specs=[hbm] * 6,
        out_specs=(pl.BlockSpec(memory_space=pltpu.VMEM),) * 3,
        scratch_shapes=[
            vmem((2, 2, COLS, WIDTH), bf), vmem((2, 2, COLS, WIDTH), bf), vmem((2, 2, COLS, WIDTH), bf),
            vmem((2, 2, COLS, FULL), bf), vmem((3, 3, FULL), f32), vmem((1, FULL), f32),
            vmem((2, COLS, FULL), bf), vmem((2, COLS, FULL), bf),
            vmem((HDIM, LPAD), f32), vmem((2, 2, BLK, 128), f32),
            vmem((2, BLK, 128), bf), vmem((2, BLK, 128), bf),
            vmem((2, 2, QTR, 128), bf), vmem((2, 2, QTR, 128), bf),
            vmem((2, QTR, 128), bf), vmem((2, QTR, 128), bf), vmem((2, QTR, 128), f32),
            vmem((8, SL, 128), bf), vmem((8, SL, 128), bf),
            vmem((SL, 128), bf), vmem((4, SL, 128), bf),
            vmem((8, SL, 128), bf), vmem((8, SL, 128), bf),
            dma((4,)), dma((2, 2)), dma((NP, 2, 2)), dma((NP, 2, 2)),
            dma((2,)), dma((2,)), dma((2,)), dma((2,)), dma((2,)), dma((2,)),
            dma((7,)), dma((7,)), dma((3,)), dma((3,)), dma((7,)), dma((7,)),
            dma((2, 3)), dma((2, 3)), dma((2, 4)), dma((2, 4)),
        ],
        compiler_params=pltpu.CompilerParams(
            collective_id=0, has_side_effects=True, vmem_limit_bytes=VMEM_BYTES
        ),
        name="states_and_conv",
    )(queries, key_rows, value_rows, hidden, conv_weight, conv_bias)
    return pl.pallas_call(
        attend,
        out_shape=(
            jax.ShapeDtypeStruct((2, 2, COLS, WIDTH), f32),
            jax.ShapeDtypeStruct((2, 2, COLS, HALF), bf),
        ),
        in_specs=[pl.BlockSpec(memory_space=pltpu.VMEM)] * 3,
        out_specs=(hbm, hbm),
        scratch_shapes=[
            vmem((HDIM, LPAD), bf), vmem((2, 2, COLS, WIDTH), f32), dma((3,)),
        ],
        compiler_params=pltpu.CompilerParams(vmem_limit_bytes=VMEM_BYTES),
        name="attend",
    )(*[pltpu.with_memory_space_constraint(a, pltpu.VMEM) for a in (phi, states, gated)])


def solution(mesh):
    block = P("tm", "rows", None, None)
    return jax.shard_map(
        on_device, mesh=mesh, in_specs=(block, block, block, block, P(), P()),
        out_specs=(block, block), check_vma=False,
    )
```

```python
import jax
import jax.numpy as jnp
from jax import lax
from jax.experimental import pallas as pl
from jax.experimental.pallas import tpu as pltpu
from jax.sharding import PartitionSpec as P

HEADS = 20
HDIM = 112
WIDTH = HEADS * HDIM
HALF = 2800
FULL = 2 * HALF
COLS = 80
TOK = 2 * COLS
LT = 18
LPAD = LT * 128
HT = LT // 2
BLK = 1024
TOTROW = HT * HDIM
QTR = BLK // 4
SL = QTR // 8
MESH = pl.DeviceIdType.MESH
CUTS = (0, 4, 8, 12, 16, 19, 22)
NP = len(CUTS) - 1
VMEM_BYTES = 56 * 1024 * 1024


def val_lanes(k):
    lo, hi = CUTS[k], min(CUTS[k + 1], 21)
    return lo * 128, (hi - lo) * 128


def gate_lanes(k):
    lo = 21 if k == 0 else 22 + CUTS[k]
    hi = min(22 + CUTS[k + 1], 44)
    start, end = lo * 128, min(hi * 128, FULL)
    return start, end - start


def features(x):
    x = x.astype(jnp.float32)
    return jnp.where(x > 0, x + 1.0, jnp.exp(x)).astype(jnp.bfloat16)


def kernel(
    q_hbm, k_hbm, v_hbm, h_hbm, w_hbm, b_hbm,
    final, phi_v, gat_v,
    q_v, k_v, v_v, h_v, w_v, b_v, up_v, dn_v,
    turned, state, send_c, recv_c, send_a, recv_a, own,
    send_z, recv_z, send_x, recv_x, send_e, recv_e,
    load_sem, kv_sem, halo_s, halo_r, c_s, c_r, a_s, a_r,
    z_s, z_r, x_s, x_r, e_s, e_r, g_s, g_r, f_s, f_r,
):
    tm = lax.axis_index("tm")
    row = lax.axis_index("rows")
    x, z = tm // 8, tm % 8
    y, c = row // 2, row % 2
    sib = (tm, row + 1 - 2 * c)
    above, below = (tm, (row + 7) % 8), (tm, (row + 1) % 8)
    ydev = [(tm, (y + d) % 4 * 2 + c) for d in range(4)]
    zdev = [(x * 8 + (z + d) % 8, row) for d in range(8)]
    xdev = [(((x + d) % 4) * 8 + z, row) for d in range(4)]

    def load(src, dst, sem):
        copy = pltpu.make_async_copy(src, dst, sem)
        copy.start()
        return copy

    kv = [
        (load(k_hbm.at[f], k_v.at[f], kv_sem.at[f, 0]), load(v_hbm.at[f], v_v.at[f], kv_sem.at[f, 1]))
        for f in range(2)
    ]
    load_h = load(h_hbm, h_v, load_sem.at[0])
    load_q = load(q_hbm, q_v, load_sem.at[1])
    load_w = load(w_hbm, w_v, load_sem.at[2])
    load_b = load(b_hbm, b_v.at[0], load_sem.at[3])

    barrier = pltpu.get_barrier_semaphore()
    partners = [above, below] + ydev[1:] + zdev[1:] + xdev[1:]
    for device in partners:
        pl.semaphore_signal(barrier, inc=1, device_id=device, device_id_type=MESH)

    def remote(src, dst, ss, rs, device):
        return pltpu.make_async_remote_copy(
            src_ref=src, dst_ref=dst, send_sem=ss, recv_sem=rs, device_id=device, device_id_type=MESH
        )

    def halo(k):
        copies = []
        for n, (start, size) in enumerate((val_lanes(k), gate_lanes(k))):
            lanes = pl.ds(start, size)
            copies.append(remote(h_hbm.at[:, 1, :, lanes], up_v.at[:, :, lanes],
                                 halo_s.at[k, n, 0], halo_r.at[k, n, 0], below))
            copies.append(remote(h_hbm.at[:, 0, :, lanes], dn_v.at[:, :, lanes],
                                 halo_s.at[k, n, 1], halo_r.at[k, n, 1], above))
        return copies

    halos = [halo(k) for k in range(NP)]

    def start(copies):
        for copy in copies:
            copy.start()

    core = []
    for f in range(2):
        kv[f][0].wait()
        sums = []
        for l in range(LT):
            n = min(128, WIDTH - 128 * l)
            phi = features(k_v[f, :, :, 128 * l:128 * l + n].reshape(TOK, n))
            turned[128 * l:128 * l + n] = phi.T
            sums.append(jnp.sum(phi.astype(jnp.float32), axis=0, keepdims=True))
        sums[-1] = jnp.concatenate([sums[-1], jnp.zeros((1, LPAD - WIDTH), jnp.float32)], axis=1)
        for half in range(2):
            rows = sums[half * HT:(half + 1) * HT] + [jnp.zeros((BLK - TOTROW - HT, 128), jnp.float32)]
            part = jnp.concatenate(rows, axis=0)
            state[f, half, TOTROW:] = part if f == 0 else part + state[0, half, TOTROW:]
        kv[f][1].wait()
        for m in range(HT):
            c0, c1 = 256 * m, min(256 * (m + 1), WIDTH)
            h0, h1 = c0 // HDIM, -(-c1 // HDIM)
            val = v_v[f, :, :, c0:c1].reshape(TOK, c1 - c0)
            prod = jnp.dot(turned[HDIM * h0:HDIM * h1], val, preferred_element_type=jnp.float32)
            for l in range(c0 // 128, -(-c1 // 128)):
                l0, l1 = 128 * l, min(128 * (l + 1), WIDTH)
                head = l0 // HDIM
                at = HDIM * (head - h0)
                part = prod[at:at + HDIM, l0 - c0:l1 - c0]
                if HDIM * (head + 1) < l1:
                    lane = lax.broadcasted_iota(jnp.int32, part.shape, 1)
                    part = jnp.where(lane < HDIM * (head + 1) - l0, part, prod[at + HDIM:at + 2 * HDIM, l0 - c0:l1 - c0])
                if l1 - l0 < 128:
                    part = jnp.concatenate([part, jnp.zeros((HDIM, 128 - l1 + l0), jnp.float32)], axis=1)
                half, rows = l // HT, slice(l % HT * HDIM, (l % HT + 1) * HDIM)
                state[f, half, rows] = part if f == 0 else part + state[0, half, rows]
        if f == 0:
            pl.semaphore_wait(barrier, len(partners))
            start(halos[0])
            start(halos[1])
        send_c[f] = state[f, 1 - c].astype(jnp.bfloat16)
        copy = remote(send_c.at[f], recv_c.at[f], c_s.at[f], c_r.at[f], sib)
        copy.start()
        core.append(copy)

    load_h.wait()
    load_w.wait()
    load_b.wait()
    top = jnp.where(row > 0, 1.0, 0.0)
    bottom = jnp.where(row < 7, 1.0, 0.0)
    shift = FULL - HALF - 22 * 128 + 128
    col8 = lax.broadcasted_iota(jnp.int32, (8, 128), 0)

    def place(size, n):
        at, to = lax.broadcasted_iota(jnp.int32, (size, n), 0), lax.broadcasted_iota(jnp.int32, (size, n), 1)
        return jnp.where(at == to + shift, 1.0, 0.0).astype(jnp.bfloat16)

    def conv_tile(rows, bias, weight):
        first, last = [weight[0] * top, weight[1], weight[2]], [weight[0], weight[1], weight[2] * bottom]
        edge = col8[:, :bias.shape[1]]
        outs = []
        for o, weights in ((0, first), (1, last)):
            parts = []
            for j in range(3):
                parts.append(sum(rows[o + i] * weights[i][j:j + 1] for i in range(3)))
            left = jnp.concatenate([parts[0][:72], jnp.where(edge < 7, parts[0][72:], 0.0)], axis=0)
            right = jnp.concatenate([jnp.where(edge > 0, parts[2][:8], 0.0), parts[2][8:]], axis=0)
            outs.append(parts[1] + bias + pltpu.roll(left, 1, 0) + pltpu.roll(right, COLS - 1, 0))
        return outs

    def input_rows(f, src):
        return [up_v[f, :, src], h_v[f, 0, :, src], h_v[f, 1, :, src], dn_v[f, :, src]]

    def conv_out(a, n):
        gate_at = (21 + a) * 128
        if n == 128:
            size = 256
            gate_src = pl.ds(pl.multiple_of(gate_at, 128), size)
            value_src = pl.ds(pl.multiple_of(a * 128, 128), 128)
        else:
            size = FULL - gate_at
            gate_src = pl.ds(gate_at, size)
            value_src = pl.ds(a * 128, 128)
        move = place(size, n)
        gates = []
        for f in range(2):
            rows = jnp.concatenate(input_rows(f, gate_src), axis=0)
            rows = jnp.dot(rows, move, preferred_element_type=jnp.float32)
            gates.append(conv_tile(
                [rows[i * COLS:(i + 1) * COLS] for i in range(4)],
                b_v[:, gate_src][:, shift:shift + n], [w_v[i, :, gate_src][:, shift:shift + n] for i in range(3)],
            ))
        for f in range(2):
            value = conv_tile(
                [r[:, :n].astype(jnp.float32) for r in input_rows(f, value_src)],
                b_v[:, value_src][:, :n], [w_v[i, :, value_src][:, :n] for i in range(3)],
            )
            for o in range(2):
                part = 0.5 * gates[f][o]
                gated = value[o] * (part + part * jnp.tanh(part))
                gat_v[f, o, :, pl.ds(a * 128 if n < 128 else pl.multiple_of(a * 128, 128), n)] = gated.astype(jnp.bfloat16)

    def conv(k):
        for copy in halos[k]:
            copy.wait_recv()
        if 0 < k < NP - 2:
            start(halos[k + 2])
        lo, hi = CUTS[k], min(CUTS[k + 1], 21)

        @pl.loop(lo, hi)
        def _(a):
            conv_out(a, 128)

        if CUTS[k + 1] == 22:
            conv_out(21, HALF - 21 * 128)

    def quarter(q):
        return pl.ds(pl.multiple_of(q * QTR, QTR), QTR)

    load_q.wait()
    for f in range(2):
        for r in range(2):
            phi_v[f, r] = features(q_v[f, r])

    step_a = [[], []]

    def scatter(f):
        core[f].wait_recv()
        full = state[f, c] + recv_c[f].astype(jnp.float32)
        state[f, c] = full
        send_a[f] = full.astype(jnp.bfloat16).reshape(4, QTR, 128)
        for d in (2, 1, 3):
            copy = remote(send_a.at[f, (y + d) % 4], recv_a.at[f, d - 1], a_s.at[f, d - 1], a_r.at[f, d - 1], ydev[d])
            copy.start()
            step_a[f].append(copy)

    def gather(f):
        for copy in step_a[f]:
            copy.wait_recv()
        own[f] = state[f, c, quarter(y)] + sum(recv_a[f, d].astype(jnp.float32) for d in range(3))

    scatter(1)
    start(halos[2])
    conv(0)
    conv(1)
    gather(1)

    send_z[...] = own[1].astype(jnp.bfloat16).reshape(8, SL, 128)
    step_z = []
    for d in (4, 3, 5, 2, 6, 1, 7):
        copy = remote(send_z.at[(z + d) % 8], recv_z.at[z], z_s.at[d - 1], z_r.at[d - 1], zdev[d])
        copy.start()
        step_z.append(copy)
    recv_z[z] = send_z[z]
    scatter(0)
    for copy in step_z:
        copy.wait_recv()
    send_x[...] = sum(recv_z[j].astype(jnp.float32) for j in range(8)).astype(jnp.bfloat16)
    step_x = []
    for d in (2, 1, 3):
        copy = remote(send_x, recv_x.at[x], x_s.at[d - 1], x_r.at[d - 1], xdev[d])
        copy.start()
        step_x.append(copy)
    recv_x[x] = jnp.zeros((SL, 128), jnp.bfloat16)
    conv(2)
    for copy in step_x:
        copy.wait_recv()
    running = jnp.zeros((SL, 128), jnp.float32)
    for i in range(4):
        running = running + jnp.where(i < x, recv_x[i].astype(jnp.float32), 0.0)
    for j in range(8):
        send_e[j] = running.astype(jnp.bfloat16)
        running = running + recv_z[j].astype(jnp.float32)
    step_e = []
    for d in (4, 3, 5, 2, 6, 1, 7):
        copy = remote(send_e.at[(z + d) % 8], recv_e.at[z], e_s.at[d - 1], e_r.at[d - 1], zdev[d])
        copy.start()
        step_e.append(copy)
    recv_e[z] = send_e[z]
    conv(3)
    gather(0)
    for copy in step_e:
        copy.wait_recv()

    before = recv_e[...].reshape(QTR, 128).astype(jnp.float32)
    for f in range(2):
        final[c, y, f] = (before + own[f]).astype(jnp.bfloat16)

    step_g, forwards = [], []

    def spread(q, dev, ss, rs):
        ref = final.at[c, q]
        copy = remote(ref, ref, ss, rs, dev)
        copy.start()
        return copy

    for d in (2, 1, 3):
        step_g.append(spread(y, ydev[d], g_s.at[d - 1], g_r.at[d - 1]))
    forwards.append(spread(y, sib, f_s.at[0], f_r.at[0]))
    conv(4)
    for n, d in ((1, 1), (2, 3), (0, 2)):
        step_g[n].wait_recv()
        forwards.append(spread((y + 4 - d) % 4, sib, f_s.at[d], f_r.at[d]))
    conv(5)
    for copy in forwards:
        copy.wait_recv()
    for copies in halos + step_a + [core, step_z, step_x, step_e, step_g, forwards]:
        for copy in copies:
            copy.wait_send()


def attend(phi_v, state_in, gat_v, att_out, gat_out, scaled, att_v, sem):
    copy_g = pltpu.make_async_copy(gat_v, gat_out, sem.at[0])
    copy_g.start()
    bf, f32 = jnp.bfloat16, jnp.float32
    for f in range(2):
        tails = [state_in[half, 3, f, TOTROW - 3 * QTR:].astype(f32) for half in range(2)]
        total = jnp.concatenate([tails[l // HT][l % HT:l % HT + 1] for l in range(LT)], axis=1)[:, :WIDTH]
        scaled[f] = (phi_v[f].reshape(TOK, WIDTH).astype(f32) * total).astype(bf)

    def state_tile(f, l):
        at, end, parts = l % HT * HDIM, (l % HT + 1) * HDIM, []
        while at < end:
            q, row = at // QTR, at % QTR
            n = min(end - at, QTR - row)
            parts.append(state_in[l // HT, q, f, row:row + n])
            at += n
        return jnp.concatenate(parts, axis=0)

    outs, done = [copy_g], 0
    for m in range(HT):
        c0, c1 = 256 * m, min(256 * (m + 1), WIDTH)
        h0, h1 = c0 // HDIM, -(-c1 // HDIM)
        w0, w1 = HDIM * h0 // 128 * 128, min(-(-HDIM * h1 // 128) * 128, WIDTH)
        lane = lax.broadcasted_iota(jnp.int32, (HDIM, c1 - c0), 1)
        masks = [(lane >= HDIM * h - c0) & (lane < HDIM * (h + 1) - c0) for h in range(h0, h1)]

        def stack(parts):
            before, after = HDIM * h0 - w0, w1 - HDIM * h1
            if before:
                parts = [jnp.zeros((before, c1 - c0), bf)] + parts
            if after:
                parts = parts + [jnp.zeros((after, c1 - c0), bf)]
            return jnp.concatenate(parts, axis=0)

        ones = stack([jnp.where(mask, 1.0, 0.0).astype(bf) for mask in masks])
        for f in range(2):
            block = jnp.concatenate([state_tile(f, l) for l in range(c0 // 128, -(-c1 // 128))], axis=1)[:, :c1 - c0]
            block = stack([jnp.where(mask, block, jnp.zeros_like(block)) for mask in masks])
            num = jnp.dot(phi_v[f, :, :, w0:w1].reshape(TOK, w1 - w0), block, preferred_element_type=f32)
            den = jnp.dot(scaled[f, :, w0:w1], ones, preferred_element_type=f32)
            att_v[f, :, :, c0:c1] = (num / den).reshape(2, COLS, c1 - c0)
        if m in (1, 3, 5, 7, 8):
            lanes = pl.ds(done, c1 - done)
            copy = pltpu.make_async_copy(att_v.at[:, :, :, lanes], att_out.at[:, :, :, lanes], sem.at[len(outs)])
            copy.start()
            outs.append(copy)
            done = c1
    for copy in outs:
        copy.wait()


def on_device(queries, key_rows, value_rows, hidden, conv_weight, conv_bias):
    bf, f32 = jnp.bfloat16, jnp.float32
    vmem, dma = pltpu.VMEM, pltpu.SemaphoreType.DMA
    hbm = pl.BlockSpec(memory_space=pltpu.HBM)
    states, phi, gated = pl.pallas_call(
        kernel,
        out_shape=(
            vmem((2, 4, 2, QTR, 128), bf), vmem((2, 2, COLS, WIDTH), bf), vmem((2, 2, COLS, HALF), bf),
        ),
        in_specs=[hbm] * 6,
        out_specs=(pl.BlockSpec(memory_space=pltpu.VMEM),) * 3,
        scratch_shapes=[
            vmem((2, 2, COLS, WIDTH), bf), vmem((2, 2, COLS, WIDTH), bf), vmem((2, 2, COLS, WIDTH), bf),
            vmem((2, 2, COLS, FULL), bf), vmem((3, 3, FULL), f32), vmem((1, FULL), f32),
            vmem((2, COLS, FULL), bf), vmem((2, COLS, FULL), bf),
            vmem((WIDTH, TOK), bf), vmem((2, 2, BLK, 128), f32),
            vmem((2, BLK, 128), bf), vmem((2, BLK, 128), bf),
            vmem((2, 4, QTR, 128), bf), vmem((2, 3, QTR, 128), bf), vmem((2, QTR, 128), f32),
            vmem((8, SL, 128), bf), vmem((8, SL, 128), bf),
            vmem((SL, 128), bf), vmem((4, SL, 128), bf),
            vmem((8, SL, 128), bf), vmem((8, SL, 128), bf),
            dma((4,)), dma((2, 2)), dma((NP, 2, 2)), dma((NP, 2, 2)),
            dma((2,)), dma((2,)), dma((2, 3)), dma((2, 3)),
            dma((7,)), dma((7,)), dma((3,)), dma((3,)), dma((7,)), dma((7,)),
            dma((3,)), dma((3,)), dma((4,)), dma((4,)),
        ],
        compiler_params=pltpu.CompilerParams(
            collective_id=0, has_side_effects=True, vmem_limit_bytes=VMEM_BYTES
        ),
        name="states_and_conv",
    )(queries, key_rows, value_rows, hidden, conv_weight, conv_bias)
    return pl.pallas_call(
        attend,
        out_shape=(
            jax.ShapeDtypeStruct((2, 2, COLS, WIDTH), f32),
            jax.ShapeDtypeStruct((2, 2, COLS, HALF), bf),
        ),
        in_specs=[pl.BlockSpec(memory_space=pltpu.VMEM)] * 3,
        out_specs=(hbm, hbm),
        scratch_shapes=[
            vmem((2, TOK, WIDTH), bf), vmem((2, 2, COLS, WIDTH), f32), dma((6,)),
        ],
        compiler_params=pltpu.CompilerParams(vmem_limit_bytes=VMEM_BYTES),
        name="attend",
    )(*[pltpu.with_memory_space_constraint(a, pltpu.VMEM) for a in (phi, states, gated)])


def solution(mesh):
    block = P("tm", "rows", None, None)
    return jax.shard_map(
        on_device, mesh=mesh, in_specs=(block, block, block, block, P(), P()),
        out_specs=(block, block), check_vma=False,
    )
```

```python
import jax
import jax.numpy as jnp
from jax import lax
from jax.experimental import pallas as pl
from jax.experimental.pallas import tpu as pltpu
from jax.sharding import PartitionSpec as P

HEADS = 20
HDIM = 112
WIDTH = HEADS * HDIM
HALF = 2800
FULL = 2 * HALF
COLS = 80
TOK = 2 * COLS
LT = 18
LPAD = LT * 128
HT = LT // 2
BLK = 1024
TOTROW = HT * HDIM
QTR = BLK // 4
SL = QTR // 8
MESH = pl.DeviceIdType.MESH
CUTS = (0, 4, 8, 12, 16, 20, 22)
NP = len(CUTS) - 1
VMEM_BYTES = 56 * 1024 * 1024


def val_lanes(k):
    lo, hi = CUTS[k], min(CUTS[k + 1], 21)
    return lo * 128, (hi - lo) * 128


def gate_lanes(k):
    lo = 21 if k == 0 else 22 + CUTS[k]
    hi = min(22 + CUTS[k + 1], 44)
    start, end = lo * 128, min(hi * 128, FULL)
    return start, end - start


def features(x):
    x = x.astype(jnp.float32)
    return jnp.where(x > 0, x + 1.0, jnp.exp(x)).astype(jnp.bfloat16)


def kernel(
    q_hbm, k_hbm, v_hbm, h_hbm, w_hbm, b_hbm,
    final, phi_v, gat_v,
    q_v, k_v, v_v, h_v, w_v, b_v, up_v, dn_v,
    turned, state, send_c, recv_c, send_a, recv_a, own,
    send_z, recv_z, send_x, recv_x, send_e, recv_e,
    load_sem, kv_sem, halo_s, halo_r, c_s, c_r, a_s, a_r,
    z_s, z_r, x_s, x_r, e_s, e_r, g_s, g_r, f_s, f_r,
):
    tm = lax.axis_index("tm")
    row = lax.axis_index("rows")
    x, z = tm // 8, tm % 8
    y, c = row // 2, row % 2
    sib = (tm, row + 1 - 2 * c)
    above, below = (tm, (row + 7) % 8), (tm, (row + 1) % 8)
    ydev = [(tm, (y + d) % 4 * 2 + c) for d in range(4)]
    zdev = [(x * 8 + (z + d) % 8, row) for d in range(8)]
    xdev = [(((x + d) % 4) * 8 + z, row) for d in range(4)]

    def load(src, dst, sem):
        copy = pltpu.make_async_copy(src, dst, sem)
        copy.start()
        return copy

    kv = [
        (load(k_hbm.at[f], k_v.at[f], kv_sem.at[f, 0]), load(v_hbm.at[f], v_v.at[f], kv_sem.at[f, 1]))
        for f in range(2)
    ]
    load_h = load(h_hbm, h_v, load_sem.at[0])
    load_q = load(q_hbm, q_v, load_sem.at[1])
    load_w = load(w_hbm, w_v, load_sem.at[2])
    load_b = load(b_hbm, b_v.at[0], load_sem.at[3])

    barrier = pltpu.get_barrier_semaphore()
    partners = [above, below] + ydev[1:] + zdev[1:] + xdev[1:]
    for device in partners:
        pl.semaphore_signal(barrier, inc=1, device_id=device, device_id_type=MESH)

    def remote(src, dst, ss, rs, device):
        return pltpu.make_async_remote_copy(
            src_ref=src, dst_ref=dst, send_sem=ss, recv_sem=rs, device_id=device, device_id_type=MESH
        )

    def halo(k):
        copies = []
        for n, (start, size) in enumerate((val_lanes(k), gate_lanes(k))):
            lanes = pl.ds(start, size)
            copies.append(remote(h_hbm.at[:, 1, :, lanes], up_v.at[:, :, lanes],
                                 halo_s.at[k, n, 0], halo_r.at[k, n, 0], below))
            copies.append(remote(h_hbm.at[:, 0, :, lanes], dn_v.at[:, :, lanes],
                                 halo_s.at[k, n, 1], halo_r.at[k, n, 1], above))
        return copies

    halos = [halo(k) for k in range(NP)]

    def start(copies):
        for copy in copies:
            copy.start()

    pl.semaphore_wait(barrier, len(partners))
    start(halos[0])

    core = []
    for f in range(2):
        kv[f][0].wait()
        sums = []
        for l in range(LT):
            n = min(128, WIDTH - 128 * l)
            phi = features(k_v[f, :, :, 128 * l:128 * l + n].reshape(TOK, n))
            turned[128 * l:128 * l + n] = phi.T
            sums.append(jnp.sum(phi.astype(jnp.float32), axis=0, keepdims=True))
        sums[-1] = jnp.concatenate([sums[-1], jnp.zeros((1, LPAD - WIDTH), jnp.float32)], axis=1)
        for half in range(2):
            rows = sums[half * HT:(half + 1) * HT] + [jnp.zeros((BLK - TOTROW - HT, 128), jnp.float32)]
            part = jnp.concatenate(rows, axis=0)
            state[f, half, TOTROW:] = part if f == 0 else part + state[0, half, TOTROW:]
        kv[f][1].wait()
        for m in range(HT):
            c0, c1 = 256 * m, min(256 * (m + 1), WIDTH)
            h0, h1 = c0 // HDIM, -(-c1 // HDIM)
            val = v_v[f, :, :, c0:c1].reshape(TOK, c1 - c0)
            prod = jnp.dot(turned[HDIM * h0:HDIM * h1], val, preferred_element_type=jnp.float32)
            for l in range(c0 // 128, -(-c1 // 128)):
                l0, l1 = 128 * l, min(128 * (l + 1), WIDTH)
                head = l0 // HDIM
                at = HDIM * (head - h0)
                part = prod[at:at + HDIM, l0 - c0:l1 - c0]
                if HDIM * (head + 1) < l1:
                    lane = lax.broadcasted_iota(jnp.int32, part.shape, 1)
                    part = jnp.where(lane < HDIM * (head + 1) - l0, part, prod[at + HDIM:at + 2 * HDIM, l0 - c0:l1 - c0])
                if l1 - l0 < 128:
                    part = jnp.concatenate([part, jnp.zeros((HDIM, 128 - l1 + l0), jnp.float32)], axis=1)
                half, rows = l // HT, slice(l % HT * HDIM, (l % HT + 1) * HDIM)
                state[f, half, rows] = part if f == 0 else part + state[0, half, rows]
        send_c[f] = state[f, 1 - c].astype(jnp.bfloat16)
        copy = remote(send_c.at[f], recv_c.at[f], c_s.at[f], c_r.at[f], sib)
        copy.start()
        core.append(copy)

    load_h.wait()
    load_w.wait()
    load_b.wait()
    top = jnp.where(row > 0, 1.0, 0.0)
    bottom = jnp.where(row < 7, 1.0, 0.0)
    shift = FULL - HALF - 22 * 128 + 128
    col8 = lax.broadcasted_iota(jnp.int32, (8, 128), 0)

    def place(size, n):
        at, to = lax.broadcasted_iota(jnp.int32, (size, n), 0), lax.broadcasted_iota(jnp.int32, (size, n), 1)
        return jnp.where(at == to + shift, 1.0, 0.0).astype(jnp.bfloat16)

    def conv_tile(rows, bias, weight):
        first, last = [weight[0] * top, weight[1], weight[2]], [weight[0], weight[1], weight[2] * bottom]
        edge = col8[:, :bias.shape[1]]
        outs = []
        for o, weights in ((0, first), (1, last)):
            parts = []
            for j in range(3):
                parts.append(sum(rows[o + i] * weights[i][j:j + 1] for i in range(3)))
            left = jnp.concatenate([parts[0][:72], jnp.where(edge < 7, parts[0][72:], 0.0)], axis=0)
            right = jnp.concatenate([jnp.where(edge > 0, parts[2][:8], 0.0), parts[2][8:]], axis=0)
            outs.append(parts[1] + bias + pltpu.roll(left, 1, 0) + pltpu.roll(right, COLS - 1, 0))
        return outs

    def input_rows(f, src):
        return [up_v[f, :, src], h_v[f, 0, :, src], h_v[f, 1, :, src], dn_v[f, :, src]]

    def conv_out(a, n):
        gate_at = (21 + a) * 128
        if n == 128:
            size = 256
            gate_src = pl.ds(pl.multiple_of(gate_at, 128), size)
            value_src = pl.ds(pl.multiple_of(a * 128, 128), 128)
        else:
            size = FULL - gate_at
            gate_src = pl.ds(gate_at, size)
            value_src = pl.ds(a * 128, 128)
        move = place(size, n)
        gates = []
        for f in range(2):
            rows = jnp.concatenate(input_rows(f, gate_src), axis=0)
            rows = jnp.dot(rows, move, preferred_element_type=jnp.float32)
            gates.append(conv_tile(
                [rows[i * COLS:(i + 1) * COLS] for i in range(4)],
                b_v[:, gate_src][:, shift:shift + n], [w_v[i, :, gate_src][:, shift:shift + n] for i in range(3)],
            ))
        for f in range(2):
            value = conv_tile(
                [r[:, :n].astype(jnp.float32) for r in input_rows(f, value_src)],
                b_v[:, value_src][:, :n], [w_v[i, :, value_src][:, :n] for i in range(3)],
            )
            for o in range(2):
                part = 0.5 * gates[f][o]
                gated = value[o] * (part + part * jnp.tanh(part))
                gat_v[f, o, :, pl.ds(a * 128 if n < 128 else pl.multiple_of(a * 128, 128), n)] = gated.astype(jnp.bfloat16)

    def conv(k):
        for copy in halos[k]:
            copy.wait_recv()
        lo, hi = CUTS[k], min(CUTS[k + 1], 21)

        @pl.loop(lo, hi)
        def _(a):
            conv_out(a, 128)

        if CUTS[k + 1] == 22:
            conv_out(21, HALF - 21 * 128)

    def quarter(q):
        return pl.ds(pl.multiple_of(q * QTR, QTR), QTR)

    load_q.wait()
    for f in range(2):
        for r in range(2):
            phi_v[f, r] = features(q_v[f, r])

    step_a = [[], []]

    def scatter(f):
        core[f].wait_recv()
        full = state[f, c] + recv_c[f].astype(jnp.float32)
        state[f, c] = full
        send_a[f] = full.astype(jnp.bfloat16).reshape(4, QTR, 128)
        for d in (2, 1, 3):
            copy = remote(send_a.at[f, (y + d) % 4], recv_a.at[f, d - 1], a_s.at[f, d - 1], a_r.at[f, d - 1], ydev[d])
            copy.start()
            step_a[f].append(copy)

    def gather(f):
        for copy in step_a[f]:
            copy.wait_recv()
        own[f] = state[f, c, quarter(y)] + sum(recv_a[f, d].astype(jnp.float32) for d in range(3))

    scatter(1)
    start(halos[1])
    start(halos[2])
    conv(0)
    gather(1)

    send_z[...] = own[1].astype(jnp.bfloat16).reshape(8, SL, 128)
    step_z = []
    for d in (4, 3, 5, 2, 6, 1, 7):
        copy = remote(send_z.at[(z + d) % 8], recv_z.at[z], z_s.at[d - 1], z_r.at[d - 1], zdev[d])
        copy.start()
        step_z.append(copy)
    recv_z[z] = send_z[z]
    scatter(0)
    start(halos[3])
    conv(1)
    for copy in step_z:
        copy.wait_recv()
    send_x[...] = sum(recv_z[j].astype(jnp.float32) for j in range(8)).astype(jnp.bfloat16)
    step_x = []
    for d in (2, 1, 3):
        copy = remote(send_x, recv_x.at[x], x_s.at[d - 1], x_r.at[d - 1], xdev[d])
        copy.start()
        step_x.append(copy)
    recv_x[x] = jnp.zeros((SL, 128), jnp.bfloat16)
    start(halos[4])
    for copy in step_x:
        copy.wait_recv()
    running = jnp.zeros((SL, 128), jnp.float32)
    for i in range(4):
        running = running + jnp.where(i < x, recv_x[i].astype(jnp.float32), 0.0)
    for j in range(8):
        send_e[j] = running.astype(jnp.bfloat16)
        running = running + recv_z[j].astype(jnp.float32)
    step_e = []
    for d in (4, 3, 5, 2, 6, 1, 7):
        copy = remote(send_e.at[(z + d) % 8], recv_e.at[z], e_s.at[d - 1], e_r.at[d - 1], zdev[d])
        copy.start()
        step_e.append(copy)
    recv_e[z] = send_e[z]
    conv(2)
    gather(0)
    for copy in step_e:
        copy.wait_recv()

    before = recv_e[...].reshape(QTR, 128).astype(jnp.float32)
    for f in range(2):
        final[c, y, f] = (before + own[f]).astype(jnp.bfloat16)

    step_g, forwards = [], []

    def spread(q, dev, ss, rs):
        ref = final.at[c, q]
        copy = remote(ref, ref, ss, rs, dev)
        copy.start()
        return copy

    for d in (2, 1, 3):
        step_g.append(spread(y, ydev[d], g_s.at[d - 1], g_r.at[d - 1]))
    forwards.append(spread(y, sib, f_s.at[0], f_r.at[0]))
    start(halos[5])
    conv(3)
    conv(4)
    for n, d in ((1, 1), (2, 3), (0, 2)):
        step_g[n].wait_recv()
        forwards.append(spread((y + 4 - d) % 4, sib, f_s.at[d], f_r.at[d]))
    conv(5)
    for copy in forwards:
        copy.wait_recv()
    for copies in halos + step_a + [core, step_z, step_x, step_e, step_g, forwards]:
        for copy in copies:
            copy.wait_send()


def attend(phi_v, state_in, gat_v, att_out, gat_out, scaled, att_v, sem):
    copy_g = pltpu.make_async_copy(gat_v, gat_out, sem.at[0])
    copy_g.start()
    bf, f32 = jnp.bfloat16, jnp.float32
    for f in range(2):
        tails = [state_in[half, 3, f, TOTROW - 3 * QTR:].astype(f32) for half in range(2)]
        total = jnp.concatenate([tails[l // HT][l % HT:l % HT + 1] for l in range(LT)], axis=1)[:, :WIDTH]
        scaled[f] = (phi_v[f].reshape(TOK, WIDTH).astype(f32) * total).astype(bf)

    def state_tile(f, l):
        at, end, parts = l % HT * HDIM, (l % HT + 1) * HDIM, []
        while at < end:
            q, row = at // QTR, at % QTR
            n = min(end - at, QTR - row)
            parts.append(state_in[l // HT, q, f, row:row + n])
            at += n
        return jnp.concatenate(parts, axis=0)

    outs, done = [copy_g], 0
    for m in range(HT):
        c0, c1 = 256 * m, min(256 * (m + 1), WIDTH)
        h0, h1 = c0 // HDIM, -(-c1 // HDIM)
        w0, w1 = HDIM * h0 // 128 * 128, min(-(-HDIM * h1 // 128) * 128, WIDTH)
        lane = lax.broadcasted_iota(jnp.int32, (HDIM, c1 - c0), 1)
        masks = [(lane >= HDIM * h - c0) & (lane < HDIM * (h + 1) - c0) for h in range(h0, h1)]

        def stack(parts):
            before, after = HDIM * h0 - w0, w1 - HDIM * h1
            if before:
                parts = [jnp.zeros((before, c1 - c0), bf)] + parts
            if after:
                parts = parts + [jnp.zeros((after, c1 - c0), bf)]
            return jnp.concatenate(parts, axis=0)

        ones = stack([jnp.where(mask, 1.0, 0.0).astype(bf) for mask in masks])
        for f in range(2):
            block = jnp.concatenate([state_tile(f, l) for l in range(c0 // 128, -(-c1 // 128))], axis=1)[:, :c1 - c0]
            block = stack([jnp.where(mask, block, jnp.zeros_like(block)) for mask in masks])
            num = jnp.dot(phi_v[f, :, :, w0:w1].reshape(TOK, w1 - w0), block, preferred_element_type=f32)
            den = jnp.dot(scaled[f, :, w0:w1], ones, preferred_element_type=f32)
            att_v[f, :, :, c0:c1] = (num / den).reshape(2, COLS, c1 - c0)
        if m in (1, 3, 5, 7, 8):
            lanes = pl.ds(done, c1 - done)
            copy = pltpu.make_async_copy(att_v.at[:, :, :, lanes], att_out.at[:, :, :, lanes], sem.at[len(outs)])
            copy.start()
            outs.append(copy)
            done = c1
    for copy in outs:
        copy.wait()


def on_device(queries, key_rows, value_rows, hidden, conv_weight, conv_bias):
    bf, f32 = jnp.bfloat16, jnp.float32
    vmem, dma = pltpu.VMEM, pltpu.SemaphoreType.DMA
    hbm = pl.BlockSpec(memory_space=pltpu.HBM)
    states, phi, gated = pl.pallas_call(
        kernel,
        out_shape=(
            vmem((2, 4, 2, QTR, 128), bf), vmem((2, 2, COLS, WIDTH), bf), vmem((2, 2, COLS, HALF), bf),
        ),
        in_specs=[hbm] * 6,
        out_specs=(pl.BlockSpec(memory_space=pltpu.VMEM),) * 3,
        scratch_shapes=[
            vmem((2, 2, COLS, WIDTH), bf), vmem((2, 2, COLS, WIDTH), bf), vmem((2, 2, COLS, WIDTH), bf),
            vmem((2, 2, COLS, FULL), bf), vmem((3, 3, FULL), f32), vmem((1, FULL), f32),
            vmem((2, COLS, FULL), bf), vmem((2, COLS, FULL), bf),
            vmem((WIDTH, TOK), bf), vmem((2, 2, BLK, 128), f32),
            vmem((2, BLK, 128), bf), vmem((2, BLK, 128), bf),
            vmem((2, 4, QTR, 128), bf), vmem((2, 3, QTR, 128), bf), vmem((2, QTR, 128), f32),
            vmem((8, SL, 128), bf), vmem((8, SL, 128), bf),
            vmem((SL, 128), bf), vmem((4, SL, 128), bf),
            vmem((8, SL, 128), bf), vmem((8, SL, 128), bf),
            dma((4,)), dma((2, 2)), dma((NP, 2, 2)), dma((NP, 2, 2)),
            dma((2,)), dma((2,)), dma((2, 3)), dma((2, 3)),
            dma((7,)), dma((7,)), dma((3,)), dma((3,)), dma((7,)), dma((7,)),
            dma((3,)), dma((3,)), dma((4,)), dma((4,)),
        ],
        compiler_params=pltpu.CompilerParams(
            collective_id=0, has_side_effects=True, vmem_limit_bytes=VMEM_BYTES
        ),
        name="states_and_conv",
    )(queries, key_rows, value_rows, hidden, conv_weight, conv_bias)
    return pl.pallas_call(
        attend,
        out_shape=(
            jax.ShapeDtypeStruct((2, 2, COLS, WIDTH), f32),
            jax.ShapeDtypeStruct((2, 2, COLS, HALF), bf),
        ),
        in_specs=[pl.BlockSpec(memory_space=pltpu.VMEM)] * 3,
        out_specs=(hbm, hbm),
        scratch_shapes=[
            vmem((2, TOK, WIDTH), bf), vmem((2, 2, COLS, WIDTH), f32), dma((6,)),
        ],
        compiler_params=pltpu.CompilerParams(vmem_limit_bytes=VMEM_BYTES),
        name="attend",
    )(*[pltpu.with_memory_space_constraint(a, pltpu.VMEM) for a in (phi, states, gated)])


def solution(mesh):
    block = P("tm", "rows", None, None)
    return jax.shard_map(
        on_device, mesh=mesh, in_specs=(block, block, block, block, P(), P()),
        out_specs=(block, block), check_vma=False,
    )
```

```python
import jax
import jax.numpy as jnp
from jax import lax
from jax.experimental import pallas as pl
from jax.experimental.pallas import tpu as pltpu
from jax.sharding import PartitionSpec as P

HEADS = 20
HDIM = 112
WIDTH = HEADS * HDIM
HALF = 2800
FULL = 2 * HALF
COLS = 80
TOK = 2 * COLS
LT = 18
LPAD = LT * 128
HT = LT // 2
BLK = 1024
TOTROW = HT * HDIM
QTR = BLK // 4
SL = QTR // 8
MESH = pl.DeviceIdType.MESH
CUTS = (0, 4, 8, 12, 16, 20, 22)
NP = len(CUTS) - 1
VMEM_BYTES = 56 * 1024 * 1024


def val_lanes(k):
    lo, hi = CUTS[k], min(CUTS[k + 1], 21)
    return lo * 128, (hi - lo) * 128


def gate_lanes(k):
    lo = 21 if k == 0 else 22 + CUTS[k]
    hi = min(22 + CUTS[k + 1], 44)
    start, end = lo * 128, min(hi * 128, FULL)
    return start, end - start


def features(x):
    x = x.astype(jnp.float32)
    return jnp.where(x > 0, x + 1.0, jnp.exp(x)).astype(jnp.bfloat16)


def kernel(
    q_hbm, k_hbm, v_hbm, h_hbm, w_hbm, b_hbm,
    final, phi_v, gat_v,
    q_v, k_v, v_v, h_v, w_v, b_v, up_v, dn_v,
    turned, state, send_c, recv_c, send_a, recv_a, own,
    send_z, recv_z, send_x, recv_x, send_e, recv_e,
    load_sem, kv_sem, halo_s, halo_r, c_s, c_r, a_s, a_r,
    z_s, z_r, x_s, x_r, e_s, e_r, g_s, g_r, f_s, f_r,
):
    tm = lax.axis_index("tm")
    row = lax.axis_index("rows")
    x, z = tm // 8, tm % 8
    y, c = row // 2, row % 2
    sib = (tm, row + 1 - 2 * c)
    above, below = (tm, (row + 7) % 8), (tm, (row + 1) % 8)
    ydev = [(tm, (y + d) % 4 * 2 + c) for d in range(4)]
    zdev = [(x * 8 + (z + d) % 8, row) for d in range(8)]
    xdev = [(((x + d) % 4) * 8 + z, row) for d in range(4)]

    def load(src, dst, sem):
        copy = pltpu.make_async_copy(src, dst, sem)
        copy.start()
        return copy

    kv = [
        (load(k_hbm.at[f], k_v.at[f], kv_sem.at[f, 0]), load(v_hbm.at[f], v_v.at[f], kv_sem.at[f, 1]))
        for f in range(2)
    ]
    load_h = load(h_hbm, h_v, load_sem.at[0])
    load_q = load(q_hbm, q_v, load_sem.at[1])
    load_w = load(w_hbm, w_v, load_sem.at[2])
    load_b = load(b_hbm, b_v.at[0], load_sem.at[3])

    barrier = pltpu.get_barrier_semaphore()
    partners = [above, below] + ydev[1:] + zdev[1:] + xdev[1:]
    for device in partners:
        pl.semaphore_signal(barrier, inc=1, device_id=device, device_id_type=MESH)

    def remote(src, dst, ss, rs, device):
        return pltpu.make_async_remote_copy(
            src_ref=src, dst_ref=dst, send_sem=ss, recv_sem=rs, device_id=device, device_id_type=MESH
        )

    def halo(k):
        copies = []
        for n, (start, size) in enumerate((val_lanes(k), gate_lanes(k))):
            lanes = pl.ds(start, size)
            copies.append(remote(h_hbm.at[:, 1, :, lanes], up_v.at[:, :, lanes],
                                 halo_s.at[k, n, 0], halo_r.at[k, n, 0], below))
            copies.append(remote(h_hbm.at[:, 0, :, lanes], dn_v.at[:, :, lanes],
                                 halo_s.at[k, n, 1], halo_r.at[k, n, 1], above))
        return copies

    halos = [halo(k) for k in range(NP)]

    def each(copies, act):
        @pl.when(row < 7)
        def _():
            for copy in copies[0::2]:
                act(copy)

        @pl.when(row > 0)
        def _():
            for copy in copies[1::2]:
                act(copy)

    def start(copies):
        each(copies, lambda copy: copy.start())

    pl.semaphore_wait(barrier, len(partners))
    start(halos[0])

    core = []
    for f in range(2):
        kv[f][0].wait()
        sums = []
        for l in range(LT):
            n = min(128, WIDTH - 128 * l)
            phi = features(k_v[f, :, :, 128 * l:128 * l + n].reshape(TOK, n))
            turned[128 * l:128 * l + n] = phi.T
            sums.append(jnp.sum(phi.astype(jnp.float32), axis=0, keepdims=True))
        sums[-1] = jnp.concatenate([sums[-1], jnp.zeros((1, LPAD - WIDTH), jnp.float32)], axis=1)
        for half in range(2):
            rows = sums[half * HT:(half + 1) * HT] + [jnp.zeros((BLK - TOTROW - HT, 128), jnp.float32)]
            part = jnp.concatenate(rows, axis=0)
            state[f, half, TOTROW:] = part if f == 0 else part + state[0, half, TOTROW:]
        kv[f][1].wait()
        for m in range(HT):
            c0, c1 = 256 * m, min(256 * (m + 1), WIDTH)
            h0, h1 = c0 // HDIM, -(-c1 // HDIM)
            val = v_v[f, :, :, c0:c1].reshape(TOK, c1 - c0)
            prod = jnp.dot(turned[HDIM * h0:HDIM * h1], val, preferred_element_type=jnp.float32)
            for l in range(c0 // 128, -(-c1 // 128)):
                l0, l1 = 128 * l, min(128 * (l + 1), WIDTH)
                head = l0 // HDIM
                at = HDIM * (head - h0)
                part = prod[at:at + HDIM, l0 - c0:l1 - c0]
                if HDIM * (head + 1) < l1:
                    lane = lax.broadcasted_iota(jnp.int32, part.shape, 1)
                    part = jnp.where(lane < HDIM * (head + 1) - l0, part, prod[at + HDIM:at + 2 * HDIM, l0 - c0:l1 - c0])
                if l1 - l0 < 128:
                    part = jnp.concatenate([part, jnp.zeros((HDIM, 128 - l1 + l0), jnp.float32)], axis=1)
                half, rows = l // HT, slice(l % HT * HDIM, (l % HT + 1) * HDIM)
                state[f, half, rows] = part if f == 0 else part + state[0, half, rows]
        send_c[f] = state[f, 1 - c].astype(jnp.bfloat16)
        copy = remote(send_c.at[f], recv_c.at[f], c_s.at[f], c_r.at[f], sib)
        copy.start()
        core.append(copy)

    @pl.when(row == 0)
    def _():
        up_v[...] = jnp.zeros_like(up_v)

    @pl.when(row == 7)
    def _():
        dn_v[...] = jnp.zeros_like(dn_v)

    load_h.wait()
    load_w.wait()
    load_b.wait()
    top = jnp.where(row > 0, 1.0, 0.0)
    bottom = jnp.where(row < 7, 1.0, 0.0)
    shift = FULL - HALF - 22 * 128 + 128
    col8 = lax.broadcasted_iota(jnp.int32, (8, 128), 0)

    def place(size, n):
        at, to = lax.broadcasted_iota(jnp.int32, (size, n), 0), lax.broadcasted_iota(jnp.int32, (size, n), 1)
        return jnp.where(at == to + shift, 1.0, 0.0).astype(jnp.bfloat16)

    def conv_tile(rows, bias, weight):
        first, last = [weight[0] * top, weight[1], weight[2]], [weight[0], weight[1], weight[2] * bottom]
        edge = col8[:, :bias.shape[1]]
        outs = []
        for o, weights in ((0, first), (1, last)):
            parts = []
            for j in range(3):
                parts.append(sum(rows[o + i] * weights[i][j:j + 1] for i in range(3)))
            left = jnp.concatenate([parts[0][:72], jnp.where(edge < 7, parts[0][72:], 0.0)], axis=0)
            right = jnp.concatenate([jnp.where(edge > 0, parts[2][:8], 0.0), parts[2][8:]], axis=0)
            outs.append(parts[1] + bias + pltpu.roll(left, 1, 0) + pltpu.roll(right, COLS - 1, 0))
        return outs

    def input_rows(f, src):
        return [up_v[f, :, src], h_v[f, 0, :, src], h_v[f, 1, :, src], dn_v[f, :, src]]

    def conv_out(a, n):
        gate_at = (21 + a) * 128
        if n == 128:
            size = 256
            gate_src = pl.ds(pl.multiple_of(gate_at, 128), size)
            value_src = pl.ds(pl.multiple_of(a * 128, 128), 128)
        else:
            size = FULL - gate_at
            gate_src = pl.ds(gate_at, size)
            value_src = pl.ds(a * 128, 128)
        move = place(size, n)
        gates = []
        for f in range(2):
            rows = jnp.concatenate(input_rows(f, gate_src), axis=0)
            rows = jnp.dot(rows, move, preferred_element_type=jnp.float32)
            gates.append(conv_tile(
                [rows[i * COLS:(i + 1) * COLS] for i in range(4)],
                b_v[:, gate_src][:, shift:shift + n], [w_v[i, :, gate_src][:, shift:shift + n] for i in range(3)],
            ))
        for f in range(2):
            value = conv_tile(
                [r[:, :n].astype(jnp.float32) for r in input_rows(f, value_src)],
                b_v[:, value_src][:, :n], [w_v[i, :, value_src][:, :n] for i in range(3)],
            )
            for o in range(2):
                part = 0.5 * gates[f][o]
                gated = value[o] * (part + part * jnp.tanh(part))
                gat_v[f, o, :, pl.ds(a * 128 if n < 128 else pl.multiple_of(a * 128, 128), n)] = gated.astype(jnp.bfloat16)

    def conv(k):
        @pl.when(row > 0)
        def _():
            for copy in halos[k][0::2]:
                copy.wait_recv()

        @pl.when(row < 7)
        def _():
            for copy in halos[k][1::2]:
                copy.wait_recv()

        lo, hi = CUTS[k], min(CUTS[k + 1], 21)

        @pl.loop(lo, hi)
        def _(a):
            conv_out(a, 128)

        if CUTS[k + 1] == 22:
            conv_out(21, HALF - 21 * 128)

    def quarter(q):
        return pl.ds(pl.multiple_of(q * QTR, QTR), QTR)

    load_q.wait()
    for f in range(2):
        for r in range(2):
            phi_v[f, r] = features(q_v[f, r])

    step_a = [[], []]

    def scatter(f):
        core[f].wait_recv()
        full = state[f, c] + recv_c[f].astype(jnp.float32)
        state[f, c] = full
        send_a[f] = full.astype(jnp.bfloat16).reshape(4, QTR, 128)
        for d in (2, 1, 3):
            copy = remote(send_a.at[f, (y + d) % 4], recv_a.at[f, d - 1], a_s.at[f, d - 1], a_r.at[f, d - 1], ydev[d])
            copy.start()
            step_a[f].append(copy)

    def gather(f):
        for copy in step_a[f]:
            copy.wait_recv()
        own[f] = state[f, c, quarter(y)] + sum(recv_a[f, d].astype(jnp.float32) for d in range(3))

    scatter(1)
    start(halos[1])
    start(halos[2])
    conv(0)
    gather(1)

    send_z[...] = own[1].astype(jnp.bfloat16).reshape(8, SL, 128)
    step_z = []
    for d in (4, 3, 5, 2, 6, 1, 7):
        copy = remote(send_z.at[(z + d) % 8], recv_z.at[z], z_s.at[d - 1], z_r.at[d - 1], zdev[d])
        copy.start()
        step_z.append(copy)
    recv_z[z] = send_z[z]
    scatter(0)
    start(halos[3])
    conv(1)
    for copy in step_z:
        copy.wait_recv()
    send_x[...] = sum(recv_z[j].astype(jnp.float32) for j in range(8)).astype(jnp.bfloat16)
    step_x = []
    for d in (2, 1, 3):
        copy = remote(send_x, recv_x.at[x], x_s.at[d - 1], x_r.at[d - 1], xdev[d])
        copy.start()
        step_x.append(copy)
    recv_x[x] = jnp.zeros((SL, 128), jnp.bfloat16)
    start(halos[4])
    for copy in step_x:
        copy.wait_recv()
    running = jnp.zeros((SL, 128), jnp.float32)
    for i in range(4):
        running = running + jnp.where(i < x, recv_x[i].astype(jnp.float32), 0.0)
    for j in range(8):
        send_e[j] = running.astype(jnp.bfloat16)
        running = running + recv_z[j].astype(jnp.float32)
    step_e = []
    for d in (4, 3, 5, 2, 6, 1, 7):
        copy = remote(send_e.at[(z + d) % 8], recv_e.at[z], e_s.at[d - 1], e_r.at[d - 1], zdev[d])
        copy.start()
        step_e.append(copy)
    recv_e[z] = send_e[z]
    conv(2)
    gather(0)
    for copy in step_e:
        copy.wait_recv()

    before = recv_e[...].reshape(QTR, 128).astype(jnp.float32)
    for f in range(2):
        final[c, y, f] = (before + own[f]).astype(jnp.bfloat16)

    step_g, forwards = [], []

    def spread(q, dev, ss, rs):
        ref = final.at[c, q]
        copy = remote(ref, ref, ss, rs, dev)
        copy.start()
        return copy

    for d in (2, 1, 3):
        step_g.append(spread(y, ydev[d], g_s.at[d - 1], g_r.at[d - 1]))
    forwards.append(spread(y, sib, f_s.at[0], f_r.at[0]))
    start(halos[5])
    conv(3)
    conv(4)
    for n, d in ((1, 1), (2, 3), (0, 2)):
        step_g[n].wait_recv()
        forwards.append(spread((y + 4 - d) % 4, sib, f_s.at[d], f_r.at[d]))
    conv(5)
    for copy in forwards:
        copy.wait_recv()
    for copies in halos:
        each(copies, lambda copy: copy.wait_send())
    for copies in step_a + [core, step_z, step_x, step_e, step_g, forwards]:
        for copy in copies:
            copy.wait_send()


def attend(phi_v, state_in, gat_v, att_out, gat_out, scaled, att_v, sem):
    copy_g = pltpu.make_async_copy(gat_v, gat_out, sem.at[0])
    copy_g.start()
    bf, f32 = jnp.bfloat16, jnp.float32
    for f in range(2):
        tails = [state_in[half, 3, f, TOTROW - 3 * QTR:].astype(f32) for half in range(2)]
        total = jnp.concatenate([tails[l // HT][l % HT:l % HT + 1] for l in range(LT)], axis=1)[:, :WIDTH]
        scaled[f] = (phi_v[f].reshape(TOK, WIDTH).astype(f32) * total).astype(bf)

    def state_tile(f, l):
        at, end, parts = l % HT * HDIM, (l % HT + 1) * HDIM, []
        while at < end:
            q, row = at // QTR, at % QTR
            n = min(end - at, QTR - row)
            parts.append(state_in[l // HT, q, f, row:row + n])
            at += n
        return jnp.concatenate(parts, axis=0)

    outs, done = [copy_g], 0
    for m in range(HT):
        c0, c1 = 256 * m, min(256 * (m + 1), WIDTH)
        h0, h1 = c0 // HDIM, -(-c1 // HDIM)
        w0, w1 = HDIM * h0 // 128 * 128, min(-(-HDIM * h1 // 128) * 128, WIDTH)
        lane = lax.broadcasted_iota(jnp.int32, (HDIM, c1 - c0), 1)
        masks = [(lane >= HDIM * h - c0) & (lane < HDIM * (h + 1) - c0) for h in range(h0, h1)]

        def stack(parts):
            before, after = HDIM * h0 - w0, w1 - HDIM * h1
            if before:
                parts = [jnp.zeros((before, c1 - c0), bf)] + parts
            if after:
                parts = parts + [jnp.zeros((after, c1 - c0), bf)]
            return jnp.concatenate(parts, axis=0)

        ones = stack([jnp.where(mask, 1.0, 0.0).astype(bf) for mask in masks])
        for f in range(2):
            block = jnp.concatenate([state_tile(f, l) for l in range(c0 // 128, -(-c1 // 128))], axis=1)[:, :c1 - c0]
            block = stack([jnp.where(mask, block, jnp.zeros_like(block)) for mask in masks])
            num = jnp.dot(phi_v[f, :, :, w0:w1].reshape(TOK, w1 - w0), block, preferred_element_type=f32)
            den = jnp.dot(scaled[f, :, w0:w1], ones, preferred_element_type=f32)
            att_v[f, :, :, c0:c1] = (num / den).reshape(2, COLS, c1 - c0)
        if m in (1, 3, 5, 7, 8):
            lanes = pl.ds(done, c1 - done)
            copy = pltpu.make_async_copy(att_v.at[:, :, :, lanes], att_out.at[:, :, :, lanes], sem.at[len(outs)])
            copy.start()
            outs.append(copy)
            done = c1
    for copy in outs:
        copy.wait()


def on_device(queries, key_rows, value_rows, hidden, conv_weight, conv_bias):
    bf, f32 = jnp.bfloat16, jnp.float32
    vmem, dma = pltpu.VMEM, pltpu.SemaphoreType.DMA
    hbm = pl.BlockSpec(memory_space=pltpu.HBM)
    states, phi, gated = pl.pallas_call(
        kernel,
        out_shape=(
            vmem((2, 4, 2, QTR, 128), bf), vmem((2, 2, COLS, WIDTH), bf), vmem((2, 2, COLS, HALF), bf),
        ),
        in_specs=[hbm] * 6,
        out_specs=(pl.BlockSpec(memory_space=pltpu.VMEM),) * 3,
        scratch_shapes=[
            vmem((2, 2, COLS, WIDTH), bf), vmem((2, 2, COLS, WIDTH), bf), vmem((2, 2, COLS, WIDTH), bf),
            vmem((2, 2, COLS, FULL), bf), vmem((3, 3, FULL), f32), vmem((1, FULL), f32),
            vmem((2, COLS, FULL), bf), vmem((2, COLS, FULL), bf),
            vmem((WIDTH, TOK), bf), vmem((2, 2, BLK, 128), f32),
            vmem((2, BLK, 128), bf), vmem((2, BLK, 128), bf),
            vmem((2, 4, QTR, 128), bf), vmem((2, 3, QTR, 128), bf), vmem((2, QTR, 128), f32),
            vmem((8, SL, 128), bf), vmem((8, SL, 128), bf),
            vmem((SL, 128), bf), vmem((4, SL, 128), bf),
            vmem((8, SL, 128), bf), vmem((8, SL, 128), bf),
            dma((4,)), dma((2, 2)), dma((NP, 2, 2)), dma((NP, 2, 2)),
            dma((2,)), dma((2,)), dma((2, 3)), dma((2, 3)),
            dma((7,)), dma((7,)), dma((3,)), dma((3,)), dma((7,)), dma((7,)),
            dma((3,)), dma((3,)), dma((4,)), dma((4,)),
        ],
        compiler_params=pltpu.CompilerParams(
            collective_id=0, has_side_effects=True, vmem_limit_bytes=VMEM_BYTES
        ),
        name="states_and_conv",
    )(queries, key_rows, value_rows, hidden, conv_weight, conv_bias)
    return pl.pallas_call(
        attend,
        out_shape=(
            jax.ShapeDtypeStruct((2, 2, COLS, WIDTH), f32),
            jax.ShapeDtypeStruct((2, 2, COLS, HALF), bf),
        ),
        in_specs=[pl.BlockSpec(memory_space=pltpu.VMEM)] * 3,
        out_specs=(hbm, hbm),
        scratch_shapes=[
            vmem((2, TOK, WIDTH), bf), vmem((2, 2, COLS, WIDTH), f32), dma((6,)),
        ],
        compiler_params=pltpu.CompilerParams(vmem_limit_bytes=VMEM_BYTES),
        name="attend",
    )(*[pltpu.with_memory_space_constraint(a, pltpu.VMEM) for a in (phi, states, gated)])


def solution(mesh):
    block = P("tm", "rows", None, None)
    return jax.shard_map(
        on_device, mesh=mesh, in_specs=(block, block, block, block, P(), P()),
        out_specs=(block, block), check_vma=False,
    )
```
